32 devices in a mesh: row: 16 (over z, x, core), col: 2 (over y).
Axes of the slice: x: 2, y: 2, z: 4, core: 2. Of those that a mesh axis runs over, the one named last changes fastest.
Arguments:
- pending: bfloat16 [16384, 2, 1024], P('row', 'col'), may hold values from -5 to 5
- panel: bfloat16 [16384, 2, 1024], P('row', None, 'col'), may hold values from -0.1875 to 0.1875
- panel_scale: float32 [16384, 2], P('row'), may hold values from 0.1 to 1
- inverse_blocks: bfloat16 [2, 1024, 1024], P(None, 'col'), as said below
Outputs:
- remaining: bfloat16 [16384, 2, 1024], P('row', 'col')
- solved: bfloat16 [2, 1024, 1024], P(None, 'col')
The draws below stay inside these ranges and needn't reach their ends.
Inputs may be any that keep to these rules, and one draw needn't show every extreme that they name: `inverse_blocks`: each block is lower triangular with a positive diagonal, the inverse of a diagonal block of a Cholesky factor.
All inputs are finite; a program needn't handle non-finite values.
Results may differ from the reference program's by a relative error of at most 0.023.
Values may be sent and summed in bfloat16 or wider, within the bound.
No kernel may reach another device: no remote copies, remote signals or barrier semaphores. Data moves between devices by JAX's collectives and lax.ppermute only.
A program may use at most 64 MiB of HBM per device.

```python
import math
import jax
import jax.numpy as jnp
from jax import lax

NB = 1024
NRHS = 1024
R = 1
ROWS = 16384
N_ROW = 16
N_COL = 2


def draw_inverse_blocks(key, part):
    key_low = jax.random.fold_in(key, 11)
    key_diag = jax.random.fold_in(key, 23)
    lower = jax.random.normal(key_low, (2, NB, NB), jnp.float32) * (1.5 / jnp.sqrt(jnp.float32(NB)))
    diag = jnp.exp(jax.random.uniform(key_diag, (2, NB), jnp.float32, jnp.log(0.5), jnp.log(2.0)))
    index = jnp.arange(NB)
    strict = index[:, None] > index[None, :]
    eye = (index[:, None] == index[None, :]).astype(jnp.float32)
    whole = jnp.where(strict[None], lower, 0.0) + diag[:, :, None] * eye[None]
    return whole.astype(jnp.bfloat16)


def steps_of(stream_key, shape, cuts, low, top_value):
    def one(position, blocks):
        draws = jax.random.uniform(jax.random.fold_in(jax.random.fold_in(stream_key, 6), position), (blocks,), jnp.float32, low / len(cuts), top_value / len(cuts))
        return jnp.repeat(jnp.exp(draws), shape[position] // blocks).reshape((-1,) + (1,) * (len(shape) - position - 1))

    factor_of = one(*cuts[0])
    for cut in cuts[1:]:
        factor_of = factor_of * one(*cut)
    return factor_of


def normal_values(stream_key, shape, scale, limit, cuts=(), kind=jnp.bfloat16):
    entries = scale * jax.random.normal(stream_key, shape, jnp.float32)
    if cuts:
        entries = entries * steps_of(stream_key, shape, cuts, -0.22, 0.18)
    return jnp.clip(entries, -limit, limit).astype(kind)


def setup_inputs(seed: int = 0) -> dict:
    arg_keys = jax.random.split(jax.random.key(seed), 5)
    pending = normal_values(arg_keys[0], (ROWS, N_COL, NRHS), 0.35, 5.0, ((0, 16), (1, 2)))
    panel = normal_values(arg_keys[1], (ROWS, 2, NB), NB ** -0.5, 0.1875, ((0, 16), (2, 2)))
    panel_scale = jnp.clip(jnp.exp(math.log(1.0) - 2.3025851 * jax.random.uniform(arg_keys[2], (ROWS, 2), jnp.float32) ** steps_of(arg_keys[2], (ROWS, 2), ((0, 16),), -0.2, 0.2)), 0.1, 1.0)
    inverse_blocks = draw_inverse_blocks(jax.random.fold_in(arg_keys[4], 71), 0)
    return dict(pending=pending, panel=panel, panel_scale=panel_scale, inverse_blocks=inverse_blocks)


def reference(pending, panel, panel_scale, inverse_blocks):
    cols_dev = NB // N_COL
    current = pending.reshape(N_ROW, R, NB, N_COL, NRHS)
    blocks = panel.reshape(N_ROW, R, NB, 2, N_COL, cols_dev)
    scales = panel_scale.reshape(N_ROW, R, NB, 2)
    slot_ids = jnp.arange(R, dtype=jnp.int32)
    solved_list = []
    for k in range(2):
        fan = jnp.sum(current[k, 0].astype(jnp.float32), axis=1)
        fan_rounded = fan.astype(jnp.bfloat16)
        solution = jnp.dot(inverse_blocks[k], fan_rounded, preferred_element_type=jnp.float32).astype(jnp.bfloat16)
        solved_list.append(solution)
        pieces = solution.reshape(N_COL, cols_dev, NRHS).astype(jnp.float32)

        def update_row(items):
            row_index, cur, blk, scl = items
            term = jnp.einsum("sicj,cjn->sicn", blk[:, :, k].astype(jnp.float32), pieces)
            newer = (cur.astype(jnp.float32) - scl[:, :, k][:, :, None, None] * term).astype(jnp.bfloat16)
            global_ids = slot_ids * N_ROW + row_index
            keep = (global_ids > k)[:, None, None, None]
            return jnp.where(keep, newer, cur)

        current = lax.map(update_row, (jnp.arange(N_ROW, dtype=jnp.int32), current, blocks, scales))
    remaining = current.reshape(N_ROW * R * NB, N_COL, NRHS)
    return remaining, jnp.stack(solved_list)
```

```python
import jax
import jax.numpy as jnp
from jax import lax
from jax.sharding import PartitionSpec as P

AXES = ("row", "col")
BF = jnp.bfloat16


def dot(a, b):
    return jnp.dot(a, b, preferred_element_type=jnp.float32)


def device(x, c, z, k):
    return ((z * 2 + x) * 2 + k) * 2 + c


PLACES = [(x, c, z, k) for z in range(4) for x in range(2) for k in range(2) for c in range(2)]


def paired(wanted):
    mate = {}
    for a, b in wanted:
        mate[a], mate[b] = b, a

    def partners(x, c, z, k):
        return ((x, c, z, 1 - k), (1 - x, c, z, k), (x, 1 - c, z, k), (1 - x, c, z, 1 - k))

    for choice in range(4):
        for place in PLACES:
            other = partners(*place)[choice]
            if place not in mate and other not in mate:
                mate[place], mate[other] = other, place
    assert len(mate) == len(PLACES)
    return [(device(*a), device(*b)) for a, b in mate.items()]


def swap(value, wanted):
    return lax.ppermute(value, AXES, paired(wanted))


def core_swap(value):
    return swap(value, [((x, c, z, 0), (x, c, z, 1)) for x, c, z, k in PLACES if k == 0])


def fan_out(solved, core, x, z, k):
    half = solved.shape[1] // 2
    left, right = solved[:, :half], solved[:, half:]
    hop = swap(right, [((0, c, 0, core), (1, c, 0, core)) for c in range(2)])
    mine = jnp.where(x == 0, left, hop)
    sent = [
        swap(mine, [((s, c, 0, core), (s, c, far, core)) for c in range(2) for s in range(2)])
        for far in (1, 2, 3)
    ]
    for far in (1, 2, 3):
        mine = jnp.where(z == far, sent[far - 1], mine)
    other = swap(mine, [((0, c, far, core), (1, c, far, core)) for c in range(2) for far in range(4)])
    mine = jnp.where(k == core, mine, core_swap(mine))
    other = jnp.where(k == core, other, core_swap(other))
    return jnp.concatenate(
        [jnp.where(x == 0, mine, other), jnp.where(x == 0, other, mine)], axis=1
    )


def update(current, scale, panel, solved, keep):
    newer = (current.astype(jnp.float32) - scale * dot(panel, solved)).astype(BF)
    return jnp.where(keep, newer, current)


def body(pending, panel, panel_scale, inverse_blocks):
    row, c = lax.axis_index("row"), lax.axis_index("col")
    z, x, k = row // 4, (row // 2) % 2, row % 2
    half = inverse_blocks.shape[1]
    share = pending[:, 0, :]
    top, bottom = share[:half], share[half:]
    inv0, inv1 = inverse_blocks[0], inverse_blocks[1]
    roots = [((0, 0, 0, 0), (0, 1, 0, 0))]
    seconds = [((0, 0, 0, 1), (0, 1, 0, 1))]

    far_top = swap(top, roots)
    far_bottom = swap(jnp.where(c == 0, bottom, inv1), roots)
    fan_top = (top.astype(jnp.float32) + far_top.astype(jnp.float32)).astype(BF)
    fan_bottom = (bottom.astype(jnp.float32) + far_bottom.astype(jnp.float32)).astype(BF)
    solved0 = (dot(inv0[:, :half], fan_top) + dot(inv0[:, half:], fan_bottom)).astype(BF)

    solved0_here = core_swap(solved0)
    inv1_far = core_swap(far_bottom)
    after = update(share, panel_scale[:, 0:1], panel[:, 0, :], solved0_here, True)
    message = jnp.where(c == 0, dot(inv1_far, after).astype(BF), after[:half])
    answer = swap(message, seconds)
    after_top = jnp.where(
        c == 0,
        (after[:half].astype(jnp.float32) + answer.astype(jnp.float32)).astype(BF),
        after[:half],
    )
    rest = jnp.where(c == 0, jnp.zeros_like(answer), answer).astype(jnp.float32)
    solved1 = (
        dot(inv1[:, :half], after_top) + dot(inv1[:, half:], after[half:]) + rest
    ).astype(BF)

    solved0 = fan_out(solved0, 0, x, z, k)
    solved1 = fan_out(solved1, 1, x, z, k)
    current = update(share, panel_scale[:, 0:1], panel[:, 0, :], solved0, row > 0)
    current = update(current, panel_scale[:, 1:2], panel[:, 1, :], solved1, row > 1)
    return current[:, None, :], jnp.stack([solved0, solved1])


def body_any(pending, panel, panel_scale, inverse_blocks):
    row = lax.axis_index("row")
    current = pending[:, 0, :]
    solved = []
    for k in range(2):
        fan = lax.psum(current, "col")
        local = dot(inverse_blocks[k], fan).astype(BF)
        arrived = lax.psum(jnp.where(row == k, local, jnp.zeros_like(local)), "row")
        solved.append(arrived)
        current = update(current, panel_scale[:, k : k + 1], panel[:, k, :], arrived, row > k)
    return current[:, None, :], jnp.stack(solved)


def solution(mesh):
    placed = (P("row", "col", None), P("row", None, "col"), P("row", None), P(None, "col", None))
    small = mesh.shape["row"] == 16 and mesh.shape["col"] == 2
    return jax.shard_map(
        body if small else body_any,
        mesh=mesh,
        in_specs=placed,
        out_specs=(P("row", "col", None), P(None, "col", None)),
        check_vma=False,
    )
```

```python
import jax
import jax.numpy as jnp
from jax import lax
from jax.experimental import pallas as pl
from jax.experimental.pallas import tpu as pltpu
from jax.sharding import PartitionSpec as P

AXES = ("row", "col")
BF = jnp.bfloat16
F32 = jnp.float32
VMEM_BYTES = 40 * 1024 * 1024


def dot(a, b):
    return jnp.dot(a, b, preferred_element_type=F32)


def device(x, c, z, k):
    return ((z * 2 + x) * 2 + k) * 2 + c


PLACES = [(x, c, z, k) for z in range(4) for x in range(2) for k in range(2) for c in range(2)]


def paired(wanted, side):
    mate = {}

    def join(a, b):
        assert a not in mate and b not in mate and a != b
        mate[a], mate[b] = b, a

    def across(place, axis):
        x, c, z, k = place
        return (1 - x, c, z, k) if axis == "x" else (x, 1 - c, z, k)

    def core(place):
        x, c, z, k = place
        return (x, c, z, 1 - k)

    for a, b in wanted:
        join(a, b)
    for axis in (side, "y" if side == "x" else "x"):
        for place in [p for p in PLACES if p not in mate and core(p) in mate]:
            if place not in mate and across(place, axis) not in mate:
                join(place, across(place, axis))
    for place in PLACES:
        if place not in mate:
            join(place, core(place))
    return [(device(*a), device(*b)) for a, b in mate.items()]


def swap(value, wanted, side):
    return lax.ppermute(value, AXES, paired(wanted, side))


def core_swap(value):
    return swap(value, [((x, c, z, 0), (x, c, z, 1)) for x, c, z, k in PLACES if k == 0], "x")


def fan_out(parts, core, x, z, k):
    hop = swap(parts[1], [((0, c, 0, core), (1, c, 0, core)) for c in range(2)], "y")
    mine = jnp.where(x == 0, parts[0], hop)
    sent = [
        swap(mine, [((s, c, 0, core), (s, c, far, core)) for c in range(2) for s in range(2)], "x")
        for far in (1, 2, 3)
    ]
    for far in (1, 2, 3):
        mine = jnp.where(z == far, sent[far - 1], mine)
    other = swap(mine, [((0, c, far, core), (1, c, far, core)) for c in range(2) for far in range(4)], "y")
    mine = jnp.where(k == core, mine, core_swap(mine))
    other = jnp.where(k == core, other, core_swap(other))
    return mine, other


def call(kernel, grid, ins, outs, shapes, scalars, operands, aliases=None):
    return pl.pallas_call(
        kernel,
        grid_spec=pltpu.PrefetchScalarGridSpec(
            num_scalar_prefetch=1, grid=grid, in_specs=ins, out_specs=outs
        ),
        out_shape=shapes,
        input_output_aliases=aliases or {},
        compiler_params=pltpu.CompilerParams(vmem_limit_bytes=VMEM_BYTES),
    )(scalars, *operands)


def solve_first(flags, share, far_top, far_bottom, inverse, half):
    n = share.shape[1]
    tile = half // 2

    def kernel(flags, top, bottom, far_t, far_b, inv, out):
        fan_t = (top[...].astype(F32) + far_t[...].astype(F32)).astype(BF)
        fan_b = (bottom[...].astype(F32) + far_b[...].astype(F32)).astype(BF)
        fan_b = jnp.where(flags[1] == 0, bottom[...], fan_b)
        whole = dot(inv[0, :, :half], fan_t) + dot(inv[0, :, half:], fan_b)
        out[0] = whole.astype(BF)

    block = lambda which: pl.BlockSpec((half, tile), lambda j, f: (which, j))
    return call(
        kernel,
        (n // tile,),
        [block(0), block(1), block(0), block(0), pl.BlockSpec((1, half, n), lambda j, f: (0, 0, 0))],
        pl.BlockSpec((1, half, tile), lambda j, f: (j // 2, 0, j % 2)),
        jax.ShapeDtypeStruct((2, half, half), BF),
        flags,
        (share, share, far_top, far_bottom, inverse),
    )


def second_block(flags, share, scale, panel, solved, inverse_far, half):
    n = share.shape[1]
    tile = half // 2

    def kernel(flags, cur, scl, pan, sol, inv, after, message):
        term = dot(pan[...], sol[0])
        newer = (cur[...].astype(F32) - scl[...] * term).astype(BF)
        after[...] = newer

        @pl.when(flags[1] == 0)
        def _():
            message[...] = dot(inv[...], newer).astype(BF)

        @pl.when(flags[1] != 0)
        def _():
            message[...] = newer[:half]

    return call(
        kernel,
        (n // tile,),
        [
            pl.BlockSpec((n, tile), lambda j, f: (0, j)),
            pl.BlockSpec((n, 1), lambda j, f: (0, 0)),
            pl.BlockSpec((n, half), lambda j, f: (0, 0)),
            pl.BlockSpec((1, half, tile), lambda j, f: (j // 2, 0, j % 2)),
            pl.BlockSpec((half, n), lambda j, f: (0, 0)),
        ],
        [pl.BlockSpec((n, tile), lambda j, f: (0, j)), pl.BlockSpec((half, tile), lambda j, f: (0, j))],
        [jax.ShapeDtypeStruct((n, n), BF), jax.ShapeDtypeStruct((half, n), BF)],
        flags,
        (share, scale, panel, solved, inverse_far),
    )


def solve_second(flags, after, answer, inverse, half):
    n = after.shape[1]
    tile = half // 2

    def kernel(flags, cur, ans, inv, out):
        upper = flags[1] == 0
        got = ans[...].astype(F32)
        top = cur[:half]
        top = jnp.where(upper, (top.astype(F32) + got).astype(BF), top)
        whole = dot(inv[0, :, :half], top) + dot(inv[0, :, half:], cur[half:])
        out[0] = jnp.where(upper, whole, whole + got).astype(BF)

    return call(
        kernel,
        (n // tile,),
        [
            pl.BlockSpec((n, tile), lambda j, f: (0, j)),
            pl.BlockSpec((half, tile), lambda j, f: (0, j)),
            pl.BlockSpec((1, half, n), lambda j, f: (1, 0, 0)),
        ],
        pl.BlockSpec((1, half, tile), lambda j, f: (j // 2, 0, j % 2)),
        jax.ShapeDtypeStruct((2, half, half), BF),
        flags,
        (after, answer, inverse),
    )


def update_first(flags, share, scale, panel, mine, other, half):
    n = share.shape[1]
    tile = n // 4

    def kernel(flags, cur, scl, pan, a, b, out, solved):
        j, i = pl.program_id(0), pl.program_id(1)
        rows = half // 4

        def one(sol):
            newer = (cur[...].astype(F32) - scl[...] * dot(pan[...], sol[...])).astype(BF)
            out[...] = jnp.where(flags[0] > 0, newer, cur[...])
            solved[0] = sol[pl.ds(pl.multiple_of(i * rows, rows), rows), :]

        pl.when(j == flags[2])(lambda: one(a))
        pl.when(j != flags[2])(lambda: one(b))

    whole = pl.BlockSpec((half, half), lambda j, i, f: (0, 0))
    return call(
        kernel,
        (2, 4),
        [
            pl.BlockSpec((tile, half), lambda j, i, f: (i, j)),
            pl.BlockSpec((tile, 1), lambda j, i, f: (i, 0)),
            pl.BlockSpec((tile, half), lambda j, i, f: (i, 0)),
            whole,
            whole,
        ],
        [
            pl.BlockSpec((tile, half), lambda j, i, f: (i, j)),
            pl.BlockSpec((1, half // 4, half), lambda j, i, f: (0, i, j)),
        ],
        [jax.ShapeDtypeStruct((n, n), BF), jax.ShapeDtypeStruct((2, half, n), BF)],
        flags,
        (share, scale, panel, mine, other),
    )


def update_half(flags, current, solved, scale, panel, part, half):
    n = current.shape[1]
    tile = n // 4

    def kernel(flags, cur, _, scl, pan, sol, out, solved):
        rows = half // 4
        newer = (cur[...].astype(F32) - scl[...] * dot(pan[...], sol[...])).astype(BF)
        out[...] = jnp.where(flags[0] > 1, newer, cur[...])
        start = pl.multiple_of(pl.program_id(0) * rows, rows)
        solved[0] = sol[pl.ds(start, rows), :]

    return call(
        kernel,
        (4,),
        [
            pl.BlockSpec((tile, half), lambda i, f: (i, f[2])),
            pl.BlockSpec(memory_space=pl.ANY),
            pl.BlockSpec((tile, 1), lambda i, f: (i, 0)),
            pl.BlockSpec((tile, half), lambda i, f: (i, 0)),
            pl.BlockSpec((half, half), lambda i, f: (0, 0)),
        ],
        [
            pl.BlockSpec((tile, half), lambda i, f: (i, f[2])),
            pl.BlockSpec((1, half // 4, half), lambda i, f: (1, i, f[2])),
        ],
        [jax.ShapeDtypeStruct((n, n), BF), jax.ShapeDtypeStruct((2, half, n), BF)],
        flags,
        (current, solved, scale, panel, part),
        {1: 0, 2: 1},
    )


def body(pending, panel, panel_scale, inverse_blocks):
    row, c = lax.axis_index("row"), lax.axis_index("col")
    z, x, k = row // 4, (row // 2) % 2, row % 2
    half = inverse_blocks.shape[1]
    flags = jnp.stack([row, c, x]).astype(jnp.int32)
    flipped = jnp.stack([row, c, 1 - x]).astype(jnp.int32)
    share = pending[:, 0, :]
    roots = [((0, 0, 0, 0), (0, 1, 0, 0))]
    seconds = [((0, 0, 0, 1), (0, 1, 0, 1))]

    far_top = swap(share[:half], roots, "x")
    far_bottom = swap(jnp.where(c == 0, share[half:], inverse_blocks[1]), roots, "x")
    panel0, panel1, scale0, scale1, far_top = lax.optimization_barrier(
        (panel[:, 0, :], panel[:, 1, :], panel_scale[:, 0:1], panel_scale[:, 1:2], far_top)
    )
    first = solve_first(flags, share, far_top, far_bottom, inverse_blocks, half)
    first_here = core_swap(first)
    inverse_far = core_swap(far_bottom)
    after, message = second_block(flags, share, scale0, panel0, first_here, inverse_far, half)
    answer = swap(message, seconds, "x")
    second = solve_second(flags, after, answer, inverse_blocks, half)

    mine0, other0 = fan_out(first, 0, x, z, k)
    current, solved = update_first(flags, share, scale0, panel0, mine0, other0, half)
    mine1, other1 = fan_out(second, 1, x, z, k)
    current, solved = update_half(flags, current, solved, scale1, panel1, mine1, half)
    current, solved = update_half(flipped, current, solved, scale1, panel1, other1, half)
    return current[:, None, :], solved


def body_any(pending, panel, panel_scale, inverse_blocks):
    row = lax.axis_index("row")
    current = pending[:, 0, :]
    solved = []
    for k in range(2):
        fan = lax.psum(current, "col")
        local = dot(inverse_blocks[k], fan).astype(BF)
        arrived = lax.psum(jnp.where(row == k, local, jnp.zeros_like(local)), "row")
        solved.append(arrived)
        term = dot(panel[:, k, :], arrived)
        newer = (current.astype(F32) - panel_scale[:, k : k + 1] * term).astype(BF)
        current = jnp.where(row > k, newer, current)
    return current[:, None, :], jnp.stack(solved)


def solution(mesh):
    placed = (P("row", "col", None), P("row", None, "col"), P("row", None), P(None, "col", None))
    small = mesh.shape["row"] == 16 and mesh.shape["col"] == 2
    return jax.shard_map(
        body if small else body_any,
        mesh=mesh,
        in_specs=placed,
        out_specs=(P("row", "col", None), P(None, "col", None)),
        check_vma=False,
    )
```

```python
import jax
import jax.numpy as jnp
from jax import lax
from jax.experimental import pallas as pl
from jax.experimental.pallas import tpu as pltpu
from jax.sharding import PartitionSpec as P

AXES = ("row", "col")
BF = jnp.bfloat16
F32 = jnp.float32
VMEM_BYTES = 12 * 1024 * 1024
TILE = 256


def dot(a, b):
    return jnp.dot(a, b, preferred_element_type=F32)


def after(value, *others):
    return lax.optimization_barrier((value, *others))[0]


def device(x, c, z, k):
    return ((z * 2 + x) * 2 + k) * 2 + c


PLACES = [(x, c, z, k) for z in range(4) for x in range(2) for k in range(2) for c in range(2)]


def paired(wanted, side):
    mate = {}

    def join(a, b):
        assert a not in mate and b not in mate and a != b
        mate[a], mate[b] = b, a

    def across(place, axis):
        x, c, z, k = place
        return (1 - x, c, z, k) if axis == "x" else (x, 1 - c, z, k)

    def core(place):
        x, c, z, k = place
        return (x, c, z, 1 - k)

    for a, b in wanted:
        join(a, b)
    for axis in (side, "y" if side == "x" else "x"):
        for place in [p for p in PLACES if p not in mate and core(p) in mate]:
            if place not in mate and across(place, axis) not in mate:
                join(place, across(place, axis))
    for place in PLACES:
        if place not in mate:
            join(place, core(place))
    return [(device(*a), device(*b)) for a, b in mate.items()]


def swap(value, wanted, side):
    return lax.ppermute(value, AXES, paired(wanted, side))


def swap_some(value, wanted):
    return lax.ppermute(value, AXES, [(device(*p), device(*q)) for a, b in wanted for p, q in ((a, b), (b, a))])


def send(value, wanted):
    return lax.ppermute(value, AXES, [(device(*a), device(*b)) for a, b in wanted])


def core_swap(value):
    return swap(value, [((x, c, z, 0), (x, c, z, 1)) for x, c, z, k in PLACES if k == 0], "x")


COLS = (0, 1)


def far_step(core):
    return [((x, c, 0, core), (x, c, 2, core)) for c in COLS for x in (0, 1)]


def near_step(core):
    return [((x, c, z, core), (x, c, z + 1, core)) for c in COLS for x in (0, 1) for z in (0, 2)]


def side_step(core):
    return [((0, c, z, core), (1, c, z, core)) for c in COLS for z in range(4)]


VMEM = pl.BlockSpec(memory_space=pltpu.VMEM)
SMEM = pl.BlockSpec(memory_space=pltpu.SMEM)
ANY = pl.BlockSpec(memory_space=pl.ANY)


def call(kernel, operands, shapes, ins, outs, scratch=(), aliases=None):
    return pl.pallas_call(
        kernel,
        in_specs=ins,
        out_specs=outs,
        out_shape=shapes,
        scratch_shapes=list(scratch),
        input_output_aliases=aliases or {},
        compiler_params=pltpu.CompilerParams(vmem_limit_bytes=VMEM_BYTES),
    )(*operands)


def columns(share, start):
    n = share.shape[1]
    width, parts = n // 2, 4
    rows = n // parts

    def kernel(source, target, sems):
        copies = [
            pltpu.make_async_copy(
                source.at[pl.ds(i * rows, rows), pl.ds(start, width)], target.at[pl.ds(i * rows, rows)], sems.at[i]
            )
            for i in range(parts)
        ]
        for copy in copies:
            copy.start()
        for copy in copies:
            copy.wait()

    return call(
        kernel, (share,), jax.ShapeDtypeStruct((n, width), BF), [ANY], VMEM, [pltpu.SemaphoreType.DMA((parts,))]
    )


def solve_first(flags, share, far, inverse, start):
    half, n = inverse.shape

    def kernel(flags, cur, got, inv, out):
        @pl.when(flags[0] == 0)
        def _():
            for t in range(0, half, TILE):
                here = cur[:, start + t : start + t + TILE]
                fan = (here.astype(F32) + got[:, t : t + TILE].astype(F32)).astype(BF)
                out[:, t : t + TILE] = dot(inv[...], fan).astype(BF)

    return call(
        kernel, (flags, share, far, inverse), jax.ShapeDtypeStruct((half, half), BF), [SMEM] + [VMEM] * 3, VMEM
    )


def second_block(flags, share, scale, panel, solved, matrix, start):
    half, n = matrix.shape

    def kernel(flags, cur, scl, pan, sol, mat, own, message):
        @pl.when(flags[0] == 1)
        def _():
            for t in range(0, half, TILE):
                cols = slice(t, t + TILE)
                here = cur[:, start + t : start + t + TILE]
                newer = (here.astype(F32) - scl[:, 0:1] * dot(pan[...], sol[:, cols])).astype(BF)
                product = dot(mat[...], newer).astype(BF)
                upper = flags[1] == 0
                own[:, cols] = jnp.where(upper, newer[:half], product)
                message[:, cols] = jnp.where(upper, product, newer[:half])

    return call(
        kernel,
        (flags, share, scale, panel, solved, matrix),
        [jax.ShapeDtypeStruct((half, half), BF)] * 2,
        [SMEM] + [VMEM] * 5,
        [VMEM] * 2,
    )


def solve_second(flags, right, left, inverse):
    half, n = inverse.shape

    def kernel(flags, a0, b0, a1, b1, inv, out):
        def one(a, b):
            out[...] = (a[...].astype(F32) + b[...].astype(F32)).astype(BF)

        pl.when(flags[0] == 1)(lambda: one(a0, b0))
        pl.when(flags[0] == 3)(lambda: one(a1, b1))

        @pl.when(jnp.logical_and(flags[1] == 0, jnp.logical_or(flags[0] == 1, flags[0] == 3)))
        def _():
            for t in range(0, half, TILE):
                cols = slice(t, t + TILE)
                out[:, cols] = dot(inv[:, :half], out[:, cols]).astype(BF)

    return call(
        kernel,
        (flags, *right, *left, inverse),
        jax.ShapeDtypeStruct((half, half), BF),
        [SMEM] + [VMEM] * 5,
        VMEM,
    )


def gather(pieces, target):
    rows = target.shape[0] // len(pieces)
    for i, piece in enumerate(pieces):
        target[i * rows : (i + 1) * rows] = piece[...]


def update_first(flags, share, scale, panel, mine, other):
    n, half = panel.shape
    lists = [list(some) for pair in (mine, other) for some in pair]
    counts = [len(some) for some in lists]

    def kernel(flags, cur, scl, pan, *refs):
        refs = list(refs)
        parts = [[refs.pop(0) for _ in range(count)] for count in counts]
        out, solved, sol, sems = refs
        for at, side in ((0, 1 - flags[2]), (2, flags[2])):
            pl.when(flags[3] == 0)(lambda: gather(parts[at], sol.at[side]))
            pl.when(flags[3] != 0)(lambda: gather(parts[at + 1], sol.at[side]))
        copies = [
            pltpu.make_async_copy(sol.at[s], solved.at[0, :, pl.ds(s * half, half)], sems.at[s]) for s in range(2)
        ]
        for copy in copies:
            copy.start()
        for s in range(2):
            cols = slice(s * half, (s + 1) * half)
            for t in range(0, n, TILE):
                rows = slice(t, t + TILE)
                old = cur[rows, cols]
                newer = (old.astype(F32) - scl[rows, 0:1] * dot(pan[rows], sol[s])).astype(BF)
                out[rows, cols] = jnp.where(flags[0] > 0, newer, old)
        for copy in copies:
            copy.wait()

    operands = [flags, share, scale, panel, *sum(lists, [])]
    return call(
        kernel,
        operands,
        [jax.ShapeDtypeStruct((n, n), BF), jax.ShapeDtypeStruct((2, half, n), BF)],
        [SMEM] + [VMEM] * (len(operands) - 1),
        [VMEM, ANY],
        [pltpu.VMEM((2, half, half), BF), pltpu.SemaphoreType.DMA((2,))],
    )


def update_second(flags, current, scale, panel, parts, swapped, solved, remaining=None):
    n, half = panel.shape
    steps = n // TILE
    pieces = len(parts)

    def kernel(flags, cur, scl, pan, *refs):
        mine, theirs = refs[:pieces], refs[pieces : 2 * pieces]
        out, solved, sol, tile, sems = refs[-5:]
        cols = pl.ds(pl.multiple_of(flags[2] * half, half), half)
        pl.when(flags[3] == 1)(lambda: gather(mine, sol))
        pl.when(flags[3] != 1)(lambda: gather(theirs, sol))
        copies = [pltpu.make_async_copy(sol, solved.at[1, :, cols], sems.at[steps])]
        copies[0].start()
        for i in range(steps):
            rows = slice(i * TILE, (i + 1) * TILE)
            old = cur[rows, cols]
            newer = (old.astype(F32) - scl[rows, 1:2] * dot(pan[rows], sol[...])).astype(BF)
            tile[rows] = jnp.where(flags[0] > 1, newer, old)
            copy = pltpu.make_async_copy(tile.at[rows], out.at[rows, cols], sems.at[i])
            copy.start()
            copies.append(copy)
        for copy in copies:
            copy.wait()

    operands = [flags, current, scale, panel, *parts, *swapped, solved]
    aliases = {len(operands) - 1: 1}
    if remaining is not None:
        operands.append(remaining)
        aliases[len(operands) - 1] = 0
    return call(
        kernel,
        operands,
        [jax.ShapeDtypeStruct((n, n), BF), jax.ShapeDtypeStruct((2, half, n), BF)],
        [SMEM] + [VMEM] * (3 + 2 * pieces) + [ANY] * len(aliases),
        [ANY, ANY],
        [pltpu.VMEM((half, half), BF), pltpu.VMEM((n, half), BF), pltpu.SemaphoreType.DMA((steps + 1,))],
        aliases,
    )


def body(pending, panel, panel_scale, inverse_blocks):
    row, c = lax.axis_index("row"), lax.axis_index("col")
    z, x, k = lax.shift_right_logical(row, 2), lax.shift_right_logical(row, 1) & 1, row & 1
    half = inverse_blocks.shape[1]
    quarter = half // 2
    flags = jnp.stack([row, c, x, k]).astype(jnp.int32)
    flipped = jnp.stack([row, c, 1 - x, k]).astype(jnp.int32)
    roots = [((0, 0, 0, 0), (0, 1, 0, 0))]
    seconds = [((0, 0, 0, 1), (0, 1, 0, 1))]
    share, flags, flipped, upper, near, middle, odd, first_core = lax.optimization_barrier(
        (pending[:, 0, :], flags, flipped, c == 0, x == 0, z == 2, (z & 1) == 1, k == 0)
    )

    left = columns(share, 0)
    far_left = swap_some(left, roots)
    later, inverse = lax.optimization_barrier((share, inverse_blocks, left))[:2]
    inv1 = jnp.where(near, inverse[1, quarter:], inverse[1, :quarter])
    crossed = swap_some(inv1, [((1, 0, 0, 1), (1, 1, 0, 1)), ((0, 0, 1, 0), (0, 1, 1, 0))])
    panel0, panel1, later = lax.optimization_barrier((panel[:, 0, :], panel[:, 1, :], later))
    far_right = swap_some(columns(later, half), roots)
    matrix_top = send(
        crossed,
        [((1, c_, 0, 1), (0, c_, 0, 1)) for c_ in COLS] + [((0, c_, 1, 0), (0, c_, 0, 0)) for c_ in COLS],
    )
    inv0, inv1, scale = inverse[0], inverse[1], panel_scale

    first_left = solve_first(flags, share, far_left, inv0, 0)
    left_here = core_swap(first_left)
    first_hop = swap_some(first_left, [((0, c_, 0, 0), (1, c_, 0, 0)) for c_ in COLS])
    matrix_bottom = core_swap(after(matrix_top, first_left))
    matrix = jnp.where(upper, jnp.concatenate([matrix_top, matrix_bottom]), inv1)
    own, message = second_block(flags, share, scale, panel0, left_here, matrix, 0)
    own_hop = send(own, [((0, c_, 0, 1), (1, c_, 0, 1)) for c_ in COLS])
    message_hop = send(message, [((0, c_, 0, 1), (1, 1 - c_, 0, 1)) for c_ in COLS])

    first_right = solve_first(flags, share, after(far_right, own), inv0, half)
    right_here = core_swap(first_right)
    mine0 = jnp.where(near, first_right, first_hop)
    got0 = swap_some(mine0, far_step(0))
    own, message = second_block(flags, share, scale, panel0, right_here, matrix, half)
    answer = swap_some(message, seconds)

    mine0 = jnp.where(middle, got0, mine0)
    got0 = swap_some(mine0, near_step(0))

    second = solve_second(flags, (own, after(answer, mine0)), (own_hop, message_hop), inv1)

    rows = [slice(0, quarter), slice(quarter, half)]
    heads = [second[r] for r in rows]
    far = [swap(h, far_step(1), "y") for h in heads]
    mine0 = jnp.where(odd, got0, mine0)
    heads = [jnp.where(middle, f, h) for f, h in zip(far, heads)]
    step = [
        swap(jnp.where(first_core, mine0[r], h), near_step(1) + side_step(0), "y") for h, r in zip(heads, rows)
    ]
    mine1 = [jnp.where(odd, s, h) for s, h in zip(step, heads)]
    other1 = [swap(m, side_step(1), "y") for m in mine1]

    current, solved = update_first(
        flags, share, scale, panel0, ([mine0], [core_swap(mine0)]), (step, [core_swap(s) for s in step])
    )
    remaining, solved = update_second(flipped, current, scale, panel1, mine1, [core_swap(m) for m in mine1], solved)
    other1 = [after(m, remaining) for m in other1]
    remaining, solved = update_second(
        flags, current, scale, panel1, other1, [core_swap(m) for m in other1], solved, remaining
    )
    return remaining[:, None, :], solved


def body_any(pending, panel, panel_scale, inverse_blocks):
    row = lax.axis_index("row")
    current = pending[:, 0, :]
    solved = []
    for k in range(2):
        fan = lax.psum(current, "col")
        local = dot(inverse_blocks[k], fan).astype(BF)
        arrived = lax.psum(jnp.where(row == k, local, jnp.zeros_like(local)), "row")
        solved.append(arrived)
        term = dot(panel[:, k, :], arrived)
        newer = (current.astype(F32) - panel_scale[:, k : k + 1] * term).astype(BF)
        current = jnp.where(row > k, newer, current)
    return current[:, None, :], jnp.stack(solved)


def solution(mesh):
    placed = (P("row", "col", None), P("row", None, "col"), P("row", None), P(None, "col", None))
    small = mesh.shape["row"] == 16 and mesh.shape["col"] == 2
    return jax.shard_map(
        body if small else body_any,
        mesh=mesh,
        in_specs=placed,
        out_specs=(P("row", "col", None), P(None, "col", None)),
        check_vma=False,
    )
```

```python
import jax
import jax.numpy as jnp
from jax import lax
from jax.experimental import pallas as pl
from jax.experimental.pallas import tpu as pltpu
from jax.sharding import PartitionSpec as P

AXES = ("row", "col")
BF = jnp.bfloat16
F32 = jnp.float32
VMEM_BYTES = 12 * 1024 * 1024
TILE = 256


def dot(a, b):
    return jnp.dot(a, b, preferred_element_type=F32)


def after(value, *others):
    return lax.optimization_barrier((value, *others))[0]


def device(x, c, z, k):
    return ((z * 2 + x) * 2 + k) * 2 + c


PLACES = [(x, c, z, k) for z in range(4) for x in range(2) for k in range(2) for c in range(2)]


def paired(wanted, side):
    mate = {}

    def join(a, b):
        assert a not in mate and b not in mate and a != b
        mate[a], mate[b] = b, a

    def across(place, axis):
        x, c, z, k = place
        return (1 - x, c, z, k) if axis == "x" else (x, 1 - c, z, k)

    def core(place):
        x, c, z, k = place
        return (x, c, z, 1 - k)

    for a, b in wanted:
        join(a, b)
    for axis in (side, "y" if side == "x" else "x"):
        for place in [p for p in PLACES if p not in mate and core(p) in mate]:
            if place not in mate and across(place, axis) not in mate:
                join(place, across(place, axis))
    for place in PLACES:
        if place not in mate:
            join(place, core(place))
    return [(device(*a), device(*b)) for a, b in mate.items()]


def swap(value, wanted, side):
    return lax.ppermute(value, AXES, paired(wanted, side))


def swap_some(value, wanted):
    return lax.ppermute(value, AXES, [(device(*p), device(*q)) for a, b in wanted for p, q in ((a, b), (b, a))])


def send(value, wanted):
    return lax.ppermute(value, AXES, [(device(*a), device(*b)) for a, b in wanted])


def core_swap(value):
    return swap(value, [((x, c, z, 0), (x, c, z, 1)) for x, c, z, k in PLACES if k == 0], "x")


COLS = (0, 1)


def far_step(core):
    return [((x, c, 0, core), (x, c, 2, core)) for c in COLS for x in (0, 1)]


def near_step(core):
    return [((x, c, z, core), (x, c, z + 1, core)) for c in COLS for x in (0, 1) for z in (0, 2)]


def side_step(core):
    return [((0, c, z, core), (1, c, z, core)) for c in COLS for z in range(4)]


VMEM = pl.BlockSpec(memory_space=pltpu.VMEM)
SMEM = pl.BlockSpec(memory_space=pltpu.SMEM)
ANY = pl.BlockSpec(memory_space=pl.ANY)


def call(kernel, operands, shapes, ins, outs, scratch=(), aliases=None):
    return pl.pallas_call(
        kernel,
        in_specs=ins,
        out_specs=outs,
        out_shape=shapes,
        scratch_shapes=list(scratch),
        input_output_aliases=aliases or {},
        compiler_params=pltpu.CompilerParams(vmem_limit_bytes=VMEM_BYTES),
    )(*operands)


def columns(share, start):
    n = share.shape[1]
    width, parts = n // 2, 4
    rows = n // parts

    def kernel(source, target, sems):
        copies = [
            pltpu.make_async_copy(
                source.at[pl.ds(i * rows, rows), pl.ds(start, width)], target.at[pl.ds(i * rows, rows)], sems.at[i]
            )
            for i in range(parts)
        ]
        for copy in copies:
            copy.start()
        for copy in copies:
            copy.wait()

    return call(
        kernel, (share,), jax.ShapeDtypeStruct((n, width), BF), [ANY], VMEM, [pltpu.SemaphoreType.DMA((parts,))]
    )


def solve_first(flags, share, far, inverse, start):
    half, n = inverse.shape[1:]

    def kernel(flags, cur, got, inv, out):
        @pl.when(flags[0] == 0)
        def _():
            for t in range(0, half, TILE):
                here = cur[:, start + t : start + t + TILE]
                fan = (here.astype(F32) + got[:, t : t + TILE].astype(F32)).astype(BF)
                out[:, t : t + TILE] = dot(inv[0], fan).astype(BF)

    return call(
        kernel, (flags, share, far, inverse), jax.ShapeDtypeStruct((half, half), BF), [SMEM] + [VMEM] * 3, VMEM
    )


def second_block(flags, share, scale, panel, solved, inverse, far_top, far_bottom, start):
    half, n = inverse.shape[1:]
    quarter = half // 2

    def kernel(flags, cur, scl, pan, sol, inv, top, bottom, own, message):
        @pl.when(flags[0] == 1)
        def _():
            factor = column(scl[...], 0)
            for t in range(0, half, TILE):
                cols = slice(t, t + TILE)
                here = cur[:, start + t : start + t + TILE]
                newer = (here.astype(F32) - factor * dot(pan[...], sol[:, cols])).astype(BF)

                @pl.when(flags[1] == 0)
                def _():
                    own[:, cols] = newer[:half]
                    message[:quarter, cols] = dot(top[...], newer).astype(BF)
                    message[quarter:, cols] = dot(bottom[...], newer).astype(BF)

                @pl.when(flags[1] != 0)
                def _():
                    own[:, cols] = dot(inv[1], newer).astype(BF)
                    message[:, cols] = newer[:half]

    return call(
        kernel,
        (flags, share, scale, panel, solved, inverse, far_top, far_bottom),
        [jax.ShapeDtypeStruct((half, half), BF)] * 2,
        [SMEM] + [VMEM] * 7,
        [VMEM] * 2,
    )


def solve_second(flags, right, left, inverse):
    half, n = inverse.shape[1:]
    quarter = half // 2

    def kernel(flags, a0, b0, a1, b1, inv, upper, lower, both):
        def one(a, b):
            both[...] = (a[...].astype(F32) + b[...].astype(F32)).astype(BF)

        pl.when(flags[0] == 1)(lambda: one(a0, b0))
        pl.when(flags[0] == 3)(lambda: one(a1, b1))
        here = jnp.logical_or(flags[0] == 1, flags[0] == 3)

        @pl.when(jnp.logical_and(flags[1] == 0, here))
        def _():
            upper[...] = dot(inv[1, :quarter, :half], both[...]).astype(BF)
            lower[...] = dot(inv[1, quarter:, :half], both[...]).astype(BF)

        @pl.when(jnp.logical_and(flags[1] != 0, here))
        def _():
            upper[...] = both[:quarter]
            lower[...] = both[quarter:]

    return call(
        kernel,
        (flags, *right, *left, inverse),
        [jax.ShapeDtypeStruct((quarter, half), BF)] * 2,
        [SMEM] + [VMEM] * 5,
        [VMEM] * 2,
        [pltpu.VMEM((half, half), BF)],
    )


def column(scale, which):
    return jnp.transpose(jnp.concatenate([scale] * 4))[:, which : which + 1]


def gather(pieces, target):
    rows = target.shape[0] // len(pieces)
    for i, piece in enumerate(pieces):
        target[i * rows : (i + 1) * rows] = piece[...]


def update_first(flags, share, scale, panel, mine, other):
    n, half = panel.shape
    lists = [list(some) for pair in (mine, other) for some in pair]
    counts = [len(some) for some in lists]

    def kernel(flags, cur, scl, pan, *refs):
        refs = list(refs)
        parts = [[refs.pop(0) for _ in range(count)] for count in counts]
        out, solved, sol, sems = refs
        for at, side in ((0, 1 - flags[2]), (2, flags[2])):
            pl.when(flags[3] == 0)(lambda: gather(parts[at], sol.at[side]))
            pl.when(flags[3] != 0)(lambda: gather(parts[at + 1], sol.at[side]))
        copies = [
            pltpu.make_async_copy(sol.at[s], solved.at[0, :, pl.ds(s * half, half)], sems.at[s]) for s in range(2)
        ]
        for copy in copies:
            copy.start()
        factor = column(scl[...], 0)
        for s in range(2):
            cols = slice(s * half, (s + 1) * half)
            for t in range(0, n, TILE):
                rows = slice(t, t + TILE)
                old = cur[rows, cols]
                newer = (old.astype(F32) - factor[rows] * dot(pan[rows], sol[s])).astype(BF)
                out[rows, cols] = jnp.where(flags[0] > 0, newer, old)
        for copy in copies:
            copy.wait()

    operands = [flags, share, scale, panel, *sum(lists, [])]
    return call(
        kernel,
        operands,
        [jax.ShapeDtypeStruct((n, n), BF), jax.ShapeDtypeStruct((2, half, n), BF)],
        [SMEM] + [VMEM] * (len(operands) - 1),
        [VMEM, ANY],
        [pltpu.VMEM((2, half, half), BF), pltpu.SemaphoreType.DMA((2,))],
    )


def update_second(flags, current, scale, panel, parts, swapped, solved, remaining=None):
    n, half = panel.shape
    steps = n // TILE
    pieces = len(parts)

    def kernel(flags, cur, scl, pan, *refs):
        mine, theirs = refs[:pieces], refs[pieces : 2 * pieces]
        out, solved, sol, tile, sems = refs[-5:]
        cols = pl.ds(pl.multiple_of(flags[2] * half, half), half)
        pl.when(flags[3] == 1)(lambda: gather(mine, sol))
        pl.when(flags[3] != 1)(lambda: gather(theirs, sol))
        copies = [pltpu.make_async_copy(sol, solved.at[1, :, cols], sems.at[steps])]
        copies[0].start()
        factor = column(scl[...], 1)
        for i in range(steps):
            rows = slice(i * TILE, (i + 1) * TILE)
            old = cur[rows, cols]
            newer = (old.astype(F32) - factor[rows] * dot(pan[rows], sol[...])).astype(BF)
            tile[rows] = jnp.where(flags[0] > 1, newer, old)
            copy = pltpu.make_async_copy(tile.at[rows], out.at[rows, cols], sems.at[i])
            copy.start()
            copies.append(copy)
        for copy in copies:
            copy.wait()

    operands = [flags, current, scale, panel, *parts, *swapped, solved]
    aliases = {len(operands) - 1: 1}
    if remaining is not None:
        operands.append(remaining)
        aliases[len(operands) - 1] = 0
    return call(
        kernel,
        operands,
        [jax.ShapeDtypeStruct((n, n), BF), jax.ShapeDtypeStruct((2, half, n), BF)],
        [SMEM] + [VMEM] * (3 + 2 * pieces) + [ANY] * len(aliases),
        [ANY, ANY],
        [pltpu.VMEM((half, half), BF), pltpu.VMEM((n, half), BF), pltpu.SemaphoreType.DMA((steps + 1,))],
        aliases,
    )


def body(pending, panel, panel_scale, inverse_blocks):
    row, c = lax.axis_index("row"), lax.axis_index("col")
    z, x, k = lax.shift_right_logical(row, 2), lax.shift_right_logical(row, 1) & 1, row & 1
    half = inverse_blocks.shape[1]
    quarter = half // 2
    flags = jnp.stack([row, c, x, k]).astype(jnp.int32)
    flipped = jnp.stack([row, c, 1 - x, k]).astype(jnp.int32)
    roots = [((0, 0, 0, 0), (0, 1, 0, 0))]
    seconds = [((0, 0, 0, 1), (0, 1, 0, 1))]
    share, flags, flipped, near, middle, odd, outer, first_core = lax.optimization_barrier(
        (pending[:, 0, :], flags, flipped, x == 0, z == 2, (z & 1) == 1, z == 3, k == 0)
    )

    left = columns(share, 0)
    far_left = swap_some(left, roots)
    later, inverse = lax.optimization_barrier((share, inverse_blocks, left))[:2]
    rows = jnp.where(near, inverse[1, quarter:], inverse[1, :quarter])
    crossed = send(rows, [((1, 1, 0, 1), (1, 0, 0, 1)), ((0, 1, 1, 1), (0, 0, 1, 1))])
    panel0, panel1, later = lax.optimization_barrier((panel[:, 0, :], panel[:, 1, :], later))
    far_right = swap_some(columns(later, half), roots)
    far_top = send(crossed, [((1, 0, 0, 1), (0, 0, 0, 1))])
    far_bottom = send(crossed, [((0, 0, 1, 1), (0, 0, 0, 1))])
    scale = panel_scale.T

    first_left = solve_first(flags, share, far_left, inverse, 0)
    left_here = core_swap(first_left)
    first_hop = swap_some(first_left, [((0, c_, 0, 0), (1, c_, 0, 0)) for c_ in COLS])
    far_top, far_bottom = lax.optimization_barrier((far_top, far_bottom, first_left))[:2]
    own, message = second_block(flags, share, scale, panel0, left_here, inverse, far_top, far_bottom, 0)

    first_right = solve_first(flags, share, after(far_right, own, first_hop), inverse, half)
    inward = send(
        jnp.where(first_core, first_right, own),
        [((0, c_, 0, 0), (0, c_, 0, 1)) for c_ in COLS] + [((0, c_, 0, 1), (1, c_, 0, 1)) for c_ in COLS],
    )
    mine0 = jnp.where(near, first_right, first_hop)
    across = send(
        jnp.where(first_core, mine0, message),
        [((x_, c_, 0, 0), (x_, c_, 2, 0)) for x_ in (0, 1) for c_ in COLS]
        + [((0, c_, 0, 1), (1, 1 - c_, 0, 1)) for c_ in COLS],
    )
    own, message = second_block(flags, share, scale, panel0, inward, inverse, far_top, far_bottom, half)
    answer = send(
        jnp.where(first_core, mine0, message),
        [((x_, c_, 0, 0), (x_, c_, 1, 0)) for x_ in (0, 1) for c_ in COLS]
        + [((0, c_, 0, 1), (0, 1 - c_, 0, 1)) for c_ in COLS],
    )
    last = send(after(across, message), [((x_, c_, 2, 0), (x_, c_, 3, 0)) for x_ in (0, 1) for c_ in COLS])

    second = solve_second(flags, (own, answer), (inward, across), inverse)

    rows = [slice(0, quarter), slice(quarter, half)]
    mine0 = jnp.where(odd, jnp.where(outer, last, answer), jnp.where(middle, across, mine0))
    far = [swap(part, far_step(1), "y") for part in second]
    heads, step, mine1, other1 = [], [], [], []
    for part, r, head in zip(far, rows, second):
        heads.append(jnp.where(middle, after(part, *heads), head))
        step.append(swap(jnp.where(first_core, mine0[r], heads[-1]), near_step(1) + side_step(0), "y"))
    for part, head in zip(step, heads):
        mine1.append(jnp.where(odd, after(part, *mine1), head))
        other1.append(swap(mine1[-1], side_step(1), "y"))
    mine0_here = core_swap(mine0)
    step_here = [core_swap(s) for s in step]

    current, solved = update_first(
        flags, share, scale, panel0, ([mine0], [mine0_here]), (step, step_here)
    )
    remaining, solved = update_second(flipped, current, scale, panel1, mine1, [core_swap(m) for m in mine1], solved)
    other1 = [after(m, remaining) for m in other1]
    remaining, solved = update_second(
        flags, current, scale, panel1, other1, [core_swap(m) for m in other1], solved, remaining
    )
    return remaining[:, None, :], solved


def body_any(pending, panel, panel_scale, inverse_blocks):
    row = lax.axis_index("row")
    current = pending[:, 0, :]
    solved = []
    for k in range(2):
        fan = lax.psum(current, "col")
        local = dot(inverse_blocks[k], fan).astype(BF)
        arrived = lax.psum(jnp.where(row == k, local, jnp.zeros_like(local)), "row")
        solved.append(arrived)
        term = dot(panel[:, k, :], arrived)
        newer = (current.astype(F32) - panel_scale[:, k : k + 1] * term).astype(BF)
        current = jnp.where(row > k, newer, current)
    return current[:, None, :], jnp.stack(solved)


def solution(mesh):
    placed = (P("row", "col", None), P("row", None, "col"), P("row", None), P(None, "col", None))
    small = mesh.shape["row"] == 16 and mesh.shape["col"] == 2
    return jax.shard_map(
        body if small else body_any,
        mesh=mesh,
        in_specs=placed,
        out_specs=(P("row", "col", None), P(None, "col", None)),
        check_vma=False,
    )
```

```python
import jax
import jax.numpy as jnp
from jax import lax
from jax.experimental import pallas as pl
from jax.experimental.pallas import tpu as pltpu
from jax.sharding import PartitionSpec as P

AXES = ("row", "col")
BF = jnp.bfloat16
F32 = jnp.float32
VMEM_BYTES = 12 * 1024 * 1024
TILE = 256


def dot(a, b):
    return jnp.dot(a, b, preferred_element_type=F32)


def after(value, *others):
    return lax.optimization_barrier((value, *others))[0]


def device(x, c, z, k):
    return ((z * 2 + x) * 2 + k) * 2 + c


PLACES = [(x, c, z, k) for z in range(4) for x in range(2) for k in range(2) for c in range(2)]


def paired(wanted, side):
    mate = {}

    def join(a, b):
        assert a not in mate and b not in mate and a != b
        mate[a], mate[b] = b, a

    def across(place, axis):
        x, c, z, k = place
        return (1 - x, c, z, k) if axis == "x" else (x, 1 - c, z, k)

    def core(place):
        x, c, z, k = place
        return (x, c, z, 1 - k)

    for a, b in wanted:
        join(a, b)
    for axis in (side, "y" if side == "x" else "x"):
        for place in [p for p in PLACES if p not in mate and core(p) in mate]:
            if place not in mate and across(place, axis) not in mate:
                join(place, across(place, axis))
    for place in PLACES:
        if place not in mate:
            join(place, core(place))
    return [(device(*a), device(*b)) for a, b in mate.items()]


def swap(value, wanted, side):
    return lax.ppermute(value, AXES, paired(wanted, side))


def swap_some(value, wanted):
    return lax.ppermute(value, AXES, [(device(*p), device(*q)) for a, b in wanted for p, q in ((a, b), (b, a))])


def send(value, wanted):
    return lax.ppermute(value, AXES, [(device(*a), device(*b)) for a, b in wanted])


def core_swap(value):
    return swap(value, [((x, c, z, 0), (x, c, z, 1)) for x, c, z, k in PLACES if k == 0], "x")


COLS = (0, 1)


def far_step(core):
    return [((x, c, 0, core), (x, c, 2, core)) for c in COLS for x in (0, 1)]


def near_step(core):
    return [((x, c, z, core), (x, c, z + 1, core)) for c in COLS for x in (0, 1) for z in (0, 2)]


def side_step(core):
    return [((0, c, z, core), (1, c, z, core)) for c in COLS for z in range(4)]


VMEM = pl.BlockSpec(memory_space=pltpu.VMEM)
SMEM = pl.BlockSpec(memory_space=pltpu.SMEM)
ANY = pl.BlockSpec(memory_space=pl.ANY)


def call(kernel, operands, shapes, ins, outs, scratch=(), aliases=None):
    return pl.pallas_call(
        kernel,
        in_specs=ins,
        out_specs=outs,
        out_shape=shapes,
        scratch_shapes=list(scratch),
        input_output_aliases=aliases or {},
        compiler_params=pltpu.CompilerParams(vmem_limit_bytes=VMEM_BYTES),
    )(*operands)


def columns(share, start):
    n = share.shape[1]
    width, parts = n // 2, 4
    rows = n // parts

    def kernel(source, target, sems):
        copies = [
            pltpu.make_async_copy(
                source.at[pl.ds(i * rows, rows), pl.ds(start, width)], target.at[pl.ds(i * rows, rows)], sems.at[i]
            )
            for i in range(parts)
        ]
        for copy in copies:
            copy.start()
        for copy in copies:
            copy.wait()

    return call(
        kernel, (share,), jax.ShapeDtypeStruct((n, width), BF), [ANY], VMEM, [pltpu.SemaphoreType.DMA((parts,))]
    )


def solve_first(flags, share, far, inverse, start):
    half, n = inverse.shape[1:]

    def kernel(flags, cur, got, inv, out):
        @pl.when(flags[0] == 0)
        def _():
            for t in range(0, half, TILE):
                here = cur[:, start + t : start + t + TILE]
                fan = (here.astype(F32) + got[:, t : t + TILE].astype(F32)).astype(BF)
                out[:, t : t + TILE] = dot(inv[0], fan).astype(BF)

    return call(
        kernel, (flags, share, far, inverse), jax.ShapeDtypeStruct((half, half), BF), [SMEM] + [VMEM] * 3, VMEM
    )


def second_block(flags, share, scale, panel, solved, inverse, far_top, far_bottom, start):
    half, n = inverse.shape[1:]
    quarter = half // 2

    def kernel(flags, cur, scl, pan, sol, inv, top, bottom, own, message):
        @pl.when(flags[0] == 1)
        def _():
            for t in range(0, half, TILE):
                cols = slice(t, t + TILE)
                here = cur[:, start + t : start + t + TILE]
                newer = (here.astype(F32) - scl[...] * dot(pan[...], sol[:, cols])).astype(BF)

                @pl.when(flags[1] == 0)
                def _():
                    own[:, cols] = newer[:half]
                    message[:quarter, cols] = dot(top[...], newer).astype(BF)
                    message[quarter:, cols] = dot(bottom[...], newer).astype(BF)

                @pl.when(flags[1] != 0)
                def _():
                    own[:, cols] = dot(inv[1], newer).astype(BF)
                    message[:, cols] = newer[:half]

    return call(
        kernel,
        (flags, share, scale, panel, solved, inverse, far_top, far_bottom),
        [jax.ShapeDtypeStruct((half, half), BF)] * 2,
        [SMEM] + [VMEM] * 7,
        [VMEM] * 2,
    )


def solve_second(flags, right, left, inverse):
    half, n = inverse.shape[1:]
    quarter = half // 2

    def kernel(flags, a0, b0, a1, b1, inv, upper, lower, both):
        def one(a, b):
            both[...] = (a[...].astype(F32) + b[...].astype(F32)).astype(BF)

        pl.when(flags[0] == 1)(lambda: one(a0, b0))
        pl.when(flags[0] == 3)(lambda: one(a1, b1))
        here = jnp.logical_or(flags[0] == 1, flags[0] == 3)

        @pl.when(jnp.logical_and(flags[1] == 0, here))
        def _():
            upper[...] = dot(inv[1, :quarter, :half], both[...]).astype(BF)
            lower[...] = dot(inv[1, quarter:, :half], both[...]).astype(BF)

        @pl.when(jnp.logical_and(flags[1] != 0, here))
        def _():
            upper[...] = both[:quarter]
            lower[...] = both[quarter:]

    return call(
        kernel,
        (flags, *right, *left, inverse),
        [jax.ShapeDtypeStruct((quarter, half), BF)] * 2,
        [SMEM] + [VMEM] * 5,
        [VMEM] * 2,
        [pltpu.VMEM((half, half), BF)],
    )


def scale_columns(scale):
    n = scale.shape[1]

    def kernel(scl, first, second):
        both = jnp.transpose(jnp.concatenate([scl[...]] * 4))
        first[...] = both[:, 0:1]
        second[...] = both[:, 1:2]

    return call(kernel, (scale,), [jax.ShapeDtypeStruct((n, 1), F32)] * 2, [VMEM], [VMEM] * 2)


def gather(pieces, target):
    rows = target.shape[0] // len(pieces)
    for i, piece in enumerate(pieces):
        target[i * rows : (i + 1) * rows] = piece[...]


def update_first(flags, share, scale, panel, mine, other):
    n, half = panel.shape
    lists = [list(some) for pair in (mine, other) for some in pair]
    counts = [len(some) for some in lists]

    def kernel(flags, cur, scl, pan, *refs):
        refs = list(refs)
        parts = [[refs.pop(0) for _ in range(count)] for count in counts]
        out, solved, sol, sems = refs
        for at, side in ((0, 1 - flags[2]), (2, flags[2])):
            pl.when(flags[3] == 0)(lambda: gather(parts[at], sol.at[side]))
            pl.when(flags[3] != 0)(lambda: gather(parts[at + 1], sol.at[side]))
        copies = [
            pltpu.make_async_copy(sol.at[s], solved.at[0, :, pl.ds(s * half, half)], sems.at[s]) for s in range(2)
        ]
        for copy in copies:
            copy.start()
        for s in range(2):
            cols = slice(s * half, (s + 1) * half)
            for t in range(0, n, TILE):
                rows = slice(t, t + TILE)
                old = cur[rows, cols]
                newer = (old.astype(F32) - scl[rows] * dot(pan[rows], sol[s])).astype(BF)
                out[rows, cols] = jnp.where(flags[0] > 0, newer, old)
        for copy in copies:
            copy.wait()

    operands = [flags, share, scale, panel, *sum(lists, [])]
    return call(
        kernel,
        operands,
        [jax.ShapeDtypeStruct((n, n), BF), jax.ShapeDtypeStruct((2, half, n), BF)],
        [SMEM] + [VMEM] * (len(operands) - 1),
        [VMEM, ANY],
        [pltpu.VMEM((2, half, half), BF), pltpu.SemaphoreType.DMA((2,))],
    )


def update_second(flags, current, scale, panel, parts, swapped, solved, remaining=None):
    n, half = panel.shape
    steps = n // TILE
    pieces = len(parts)

    def kernel(flags, cur, scl, pan, *refs):
        mine, theirs = refs[:pieces], refs[pieces : 2 * pieces]
        out, solved, sol, tile, sems = refs[-5:]
        cols = pl.ds(pl.multiple_of(flags[2] * half, half), half)
        pl.when(flags[3] == 1)(lambda: gather(mine, sol))
        pl.when(flags[3] != 1)(lambda: gather(theirs, sol))
        copies = [pltpu.make_async_copy(sol, solved.at[1, :, cols], sems.at[steps])]
        copies[0].start()
        for i in range(steps):
            rows = slice(i * TILE, (i + 1) * TILE)
            old = cur[rows, cols]
            newer = (old.astype(F32) - scl[rows] * dot(pan[rows], sol[...])).astype(BF)
            tile[rows] = jnp.where(flags[0] > 1, newer, old)
            copy = pltpu.make_async_copy(tile.at[rows], out.at[rows, cols], sems.at[i])
            copy.start()
            copies.append(copy)
        for copy in copies:
            copy.wait()

    operands = [flags, current, scale, panel, *parts, *swapped, solved]
    aliases = {len(operands) - 1: 1}
    if remaining is not None:
        operands.append(remaining)
        aliases[len(operands) - 1] = 0
    return call(
        kernel,
        operands,
        [jax.ShapeDtypeStruct((n, n), BF), jax.ShapeDtypeStruct((2, half, n), BF)],
        [SMEM] + [VMEM] * (3 + 2 * pieces) + [ANY] * len(aliases),
        [ANY, ANY],
        [pltpu.VMEM((half, half), BF), pltpu.VMEM((n, half), BF), pltpu.SemaphoreType.DMA((steps + 1,))],
        aliases,
    )


def body(pending, panel, panel_scale, inverse_blocks):
    row, c = lax.axis_index("row"), lax.axis_index("col")
    z, x, k = lax.shift_right_logical(row, 2), lax.shift_right_logical(row, 1) & 1, row & 1
    half = inverse_blocks.shape[1]
    quarter = half // 2
    flags = jnp.stack([row, c, x, k]).astype(jnp.int32)
    flipped = jnp.stack([row, c, 1 - x, k]).astype(jnp.int32)
    roots = [((0, 0, 0, 0), (0, 1, 0, 0))]
    seconds = [((0, 0, 0, 1), (0, 1, 0, 1))]
    share, flags, flipped, near, middle, odd, outer, first_core = lax.optimization_barrier(
        (pending[:, 0, :], flags, flipped, x == 0, z == 2, (z & 1) == 1, z == 3, k == 0)
    )

    left = columns(share, 0)
    idle = [((0, c_, 0, 1), (0, c_, 1, 1)) for c_ in COLS] + [((0, c_, 1, 0), (1, c_, 1, 0)) for c_ in COLS]
    far_left = swap(left, roots + idle, "y")
    later, inverse = lax.optimization_barrier((share, inverse_blocks, left))[:2]
    rows = jnp.where(near, inverse[1, quarter:], inverse[1, :quarter])
    crossed = send(rows, [((1, 1, 0, 1), (1, 0, 0, 1)), ((0, 1, 1, 1), (0, 0, 1, 1))])
    panel0, panel1, later = lax.optimization_barrier((panel[:, 0, :], panel[:, 1, :], later))
    far_right = swap_some(columns(later, half), roots)
    far_top = send(crossed, [((1, 0, 0, 1), (0, 0, 0, 1))])
    far_bottom = send(crossed, [((0, 0, 1, 1), (0, 0, 0, 1))])
    scale0, scale1 = scale_columns(after(panel_scale.T, panel0))

    first_left = solve_first(flags, share, far_left, inverse, 0)
    left_here = core_swap(first_left)
    first_hop = send(first_left, [((0, c_, 0, 0), (1, c_, 0, 0)) for c_ in COLS])
    far_top, far_bottom = lax.optimization_barrier((far_top, far_bottom, first_left))[:2]
    own, message = second_block(flags, share, scale0, panel0, left_here, inverse, far_top, far_bottom, 0)

    first_right = solve_first(flags, share, after(far_right, own, first_hop), inverse, half)
    own_hop = send(own, [((0, c_, 0, 1), (1, c_, 0, 1)) for c_ in COLS])
    inward = core_swap(first_right)
    mine0 = lax.optimization_barrier(jnp.where(near, first_right, first_hop))
    outward = jnp.where(first_core, mine0, message)
    across = send(
        outward,
        [((x_, c_, 0, 0), (x_, c_, 2, 0)) for x_ in (0, 1) for c_ in COLS]
        + [((0, c_, 0, 1), (1, 1 - c_, 0, 1)) for c_ in COLS],
    )
    own, message = second_block(flags, share, scale0, after(panel0, outward), inward, inverse, far_top, far_bottom, half)
    answer = send(
        jnp.where(first_core, mine0, after(message, own_hop)),
        [((x_, c_, 0, 0), (x_, c_, 1, 0)) for x_ in (0, 1) for c_ in COLS]
        + [((0, c_, 0, 1), (0, 1 - c_, 0, 1)) for c_ in COLS],
    )
    last = send(after(across, message), [((x_, c_, 2, 0), (x_, c_, 3, 0)) for x_ in (0, 1) for c_ in COLS])

    second = solve_second(flags, (own, answer), (own_hop, across), inverse)

    rows = [slice(0, quarter), slice(quarter, half)]
    mine0 = jnp.where(odd, jnp.where(outer, last, answer), jnp.where(middle, across, mine0))
    far, heads, step, mine1, other1 = [], [], [], [], []
    for part, r in zip(second, rows):
        far.append(swap(jnp.where(first_core, mine0[r], part), far_step(1) + side_step(0), "y"))
    for part, head in zip(far, second):
        heads.append(jnp.where(middle, after(part, *heads), head))
        step.append(swap(heads[-1], near_step(1), "y"))
    for part, head in zip(step, heads):
        mine1.append(jnp.where(odd, after(part, *mine1), head))
        other1.append(swap(mine1[-1], side_step(1), "y"))
    mine0_here = core_swap(mine0)
    far_here = [core_swap(f) for f in far]

    current, solved = update_first(
        flags, share, scale0, panel0, ([mine0], [mine0_here]), (far, far_here)
    )
    remaining, solved = update_second(flipped, current, scale1, after(panel1, other1[0]), mine1, [core_swap(m) for m in mine1], solved)
    other1 = [after(m, remaining) for m in other1]
    remaining, solved = update_second(
        flags, current, scale1, panel1, other1, [core_swap(m) for m in other1], solved, remaining
    )
    return remaining[:, None, :], solved


def body_any(pending, panel, panel_scale, inverse_blocks):
    row = lax.axis_index("row")
    current = pending[:, 0, :]
    solved = []
    for k in range(2):
        fan = lax.psum(current, "col")
        local = dot(inverse_blocks[k], fan).astype(BF)
        arrived = lax.psum(jnp.where(row == k, local, jnp.zeros_like(local)), "row")
        solved.append(arrived)
        term = dot(panel[:, k, :], arrived)
        newer = (current.astype(F32) - panel_scale[:, k : k + 1] * term).astype(BF)
        current = jnp.where(row > k, newer, current)
    return current[:, None, :], jnp.stack(solved)


def solution(mesh):
    placed = (P("row", "col", None), P("row", None, "col"), P("row", None), P(None, "col", None))
    small = mesh.shape["row"] == 16 and mesh.shape["col"] == 2
    return jax.shard_map(
        body if small else body_any,
        mesh=mesh,
        in_specs=placed,
        out_specs=(P("row", "col", None), P(None, "col", None)),
        check_vma=False,
    )
```

```python
import jax
import jax.numpy as jnp
from jax import lax
from jax.experimental import pallas as pl
from jax.experimental.pallas import tpu as pltpu
from jax.sharding import PartitionSpec as P

AXES = ("row", "col")
BF = jnp.bfloat16
F32 = jnp.float32
VMEM_BYTES = 12 * 1024 * 1024
TILE = 256


def dot(a, b):
    return jnp.dot(a, b, preferred_element_type=F32)


def after(value, *others):
    return lax.optimization_barrier((value, *others))[0]


def device(x, c, z, k):
    return ((z * 2 + x) * 2 + k) * 2 + c


PLACES = [(x, c, z, k) for z in range(4) for x in range(2) for k in range(2) for c in range(2)]


def paired(wanted, side):
    mate = {}

    def join(a, b):
        assert a not in mate and b not in mate and a != b
        mate[a], mate[b] = b, a

    def across(place, axis):
        x, c, z, k = place
        return (1 - x, c, z, k) if axis == "x" else (x, 1 - c, z, k)

    def core(place):
        x, c, z, k = place
        return (x, c, z, 1 - k)

    for a, b in wanted:
        join(a, b)
    for axis in (side, "y" if side == "x" else "x"):
        for place in [p for p in PLACES if p not in mate and core(p) in mate]:
            if place not in mate and across(place, axis) not in mate:
                join(place, across(place, axis))
    for place in PLACES:
        if place not in mate:
            join(place, core(place))
    return [(device(*a), device(*b)) for a, b in mate.items()]


def swap(value, wanted, side):
    return lax.ppermute(value, AXES, paired(wanted, side))


def swap_some(value, wanted):
    return lax.ppermute(value, AXES, [(device(*p), device(*q)) for a, b in wanted for p, q in ((a, b), (b, a))])


def send(value, wanted):
    return lax.ppermute(value, AXES, [(device(*a), device(*b)) for a, b in wanted])


def core_swap(value):
    return swap(value, [((x, c, z, 0), (x, c, z, 1)) for x, c, z, k in PLACES if k == 0], "x")


COLS = (0, 1)


def far_step(core):
    return [((x, c, 0, core), (x, c, 2, core)) for c in COLS for x in (0, 1)]


def near_step(core):
    return [((x, c, z, core), (x, c, z + 1, core)) for c in COLS for x in (0, 1) for z in (0, 2)]


def side_step(core):
    return [((0, c, z, core), (1, c, z, core)) for c in COLS for z in range(4)]


VMEM = pl.BlockSpec(memory_space=pltpu.VMEM)
SMEM = pl.BlockSpec(memory_space=pltpu.SMEM)
ANY = pl.BlockSpec(memory_space=pl.ANY)


def call(kernel, operands, shapes, ins, outs, scratch=(), aliases=None):
    return pl.pallas_call(
        kernel,
        in_specs=ins,
        out_specs=outs,
        out_shape=shapes,
        scratch_shapes=list(scratch),
        input_output_aliases=aliases or {},
        compiler_params=pltpu.CompilerParams(vmem_limit_bytes=VMEM_BYTES),
    )(*operands)


def columns(share, start):
    n = share.shape[1]
    width, parts = n // 2, 4
    rows = n // parts

    def kernel(source, target, sems):
        copies = [
            pltpu.make_async_copy(
                source.at[pl.ds(i * rows, rows), pl.ds(start, width)], target.at[pl.ds(i * rows, rows)], sems.at[i]
            )
            for i in range(parts)
        ]
        for copy in copies:
            copy.start()
        for copy in copies:
            copy.wait()

    return call(
        kernel, (share,), jax.ShapeDtypeStruct((n, width), BF), [ANY], VMEM, [pltpu.SemaphoreType.DMA((parts,))]
    )


def solve_first(flags, share, far, inverse, start):
    half, n = inverse.shape[1:]

    def kernel(flags, cur, got, inv, out):
        @pl.when(flags[0] == 0)
        def _():
            for t in range(0, half, TILE):
                here = cur[:, start + t : start + t + TILE]
                fan = (here.astype(F32) + got[:, t : t + TILE].astype(F32)).astype(BF)
                out[:, t : t + TILE] = dot(inv[0], fan).astype(BF)

    return call(
        kernel, (flags, share, far, inverse), jax.ShapeDtypeStruct((half, half), BF), [SMEM] + [VMEM] * 3, VMEM
    )


def second_block(flags, share, scale, panel, solved, inverse, far_top, far_bottom, start):
    half, n = inverse.shape[1:]
    quarter = half // 2

    def kernel(flags, cur, scl, pan, sol, inv, top, bottom, own, message):
        @pl.when(flags[0] == 1)
        def _():
            for t in range(0, half, TILE):
                cols = slice(t, t + TILE)
                here = cur[:, start + t : start + t + TILE]
                newer = (here.astype(F32) - scl[...] * dot(pan[...], sol[:, cols])).astype(BF)

                @pl.when(flags[1] == 0)
                def _():
                    own[:, cols] = newer[:half]
                    message[:quarter, cols] = dot(top[...], newer).astype(BF)
                    message[quarter:, cols] = dot(bottom[...], newer).astype(BF)

                @pl.when(flags[1] != 0)
                def _():
                    own[:, cols] = dot(inv[1], newer).astype(BF)
                    message[:, cols] = newer[:half]

    return call(
        kernel,
        (flags, share, scale, panel, solved, inverse, far_top, far_bottom),
        [jax.ShapeDtypeStruct((half, half), BF)] * 2,
        [SMEM] + [VMEM] * 7,
        [VMEM] * 2,
    )


def solve_second(flags, right, left, inverse):
    half, n = inverse.shape[1:]
    quarter = half // 2

    def kernel(flags, a0, b0, a1, b1, inv, upper, lower, both):
        def one(a, b):
            both[...] = (a[...].astype(F32) + b[...].astype(F32)).astype(BF)

        pl.when(flags[0] == 1)(lambda: one(a0, b0))
        pl.when(flags[0] == 3)(lambda: one(a1, b1))
        here = jnp.logical_or(flags[0] == 1, flags[0] == 3)

        @pl.when(jnp.logical_and(flags[1] == 0, here))
        def _():
            upper[...] = dot(inv[1, :quarter, :half], both[...]).astype(BF)
            lower[...] = dot(inv[1, quarter:, :half], both[...]).astype(BF)

        @pl.when(jnp.logical_and(flags[1] != 0, here))
        def _():
            upper[...] = both[:quarter]
            lower[...] = both[quarter:]

    return call(
        kernel,
        (flags, *right, *left, inverse),
        [jax.ShapeDtypeStruct((quarter, half), BF)] * 2,
        [SMEM] + [VMEM] * 5,
        [VMEM] * 2,
        [pltpu.VMEM((half, half), BF)],
    )


def scale_columns(scale):
    n = scale.shape[1]

    def kernel(scl, first, second):
        both = jnp.transpose(jnp.concatenate([scl[...]] * 4))
        first[...] = both[:, 0:1]
        second[...] = both[:, 1:2]

    return call(kernel, (scale,), [jax.ShapeDtypeStruct((n, 1), F32)] * 2, [VMEM], [VMEM] * 2)


def gather(pieces, target):
    rows = target.shape[0] // len(pieces)
    for i, piece in enumerate(pieces):
        target[i * rows : (i + 1) * rows] = piece[...]


def update_first(flags, share, scale, panel, mine, other):
    n, half = panel.shape
    lists = [list(some) for pair in (mine, other) for some in pair]
    counts = [len(some) for some in lists]

    def kernel(flags, cur, scl, pan, *refs):
        refs = list(refs)
        parts = [[refs.pop(0) for _ in range(count)] for count in counts]
        out, solved, sol, sems = refs
        for at, side in ((0, 1 - flags[2]), (2, flags[2])):
            pl.when(flags[3] == 0)(lambda: gather(parts[at], sol.at[side]))
            pl.when(flags[3] != 0)(lambda: gather(parts[at + 1], sol.at[side]))
        copies = [
            pltpu.make_async_copy(sol.at[s], solved.at[0, :, pl.ds(s * half, half)], sems.at[s]) for s in range(2)
        ]
        for copy in copies:
            copy.start()
        for s in range(2):
            cols = slice(s * half, (s + 1) * half)
            for t in range(0, n, TILE):
                rows = slice(t, t + TILE)
                old = cur[rows, cols]
                newer = (old.astype(F32) - scl[rows] * dot(pan[rows], sol[s])).astype(BF)
                out[rows, cols] = jnp.where(flags[0] > 0, newer, old)
        for copy in copies:
            copy.wait()

    operands = [flags, share, scale, panel, *sum(lists, [])]
    return call(
        kernel,
        operands,
        [jax.ShapeDtypeStruct((n, n), BF), jax.ShapeDtypeStruct((2, half, n), BF)],
        [SMEM] + [VMEM] * (len(operands) - 1),
        [VMEM, ANY],
        [pltpu.VMEM((2, half, half), BF), pltpu.SemaphoreType.DMA((2,))],
    )


def update_second(flags, current, scale, panel, parts, swapped, solved, remaining=None):
    n, half = panel.shape
    steps = n // TILE
    pieces = len(parts)

    def kernel(flags, cur, scl, pan, *refs):
        mine, theirs = refs[:pieces], refs[pieces : 2 * pieces]
        out, solved, sol, tile, sems = refs[-5:]
        cols = pl.ds(pl.multiple_of(flags[2] * half, half), half)
        pl.when(flags[3] == 1)(lambda: gather(mine, sol))
        pl.when(flags[3] != 1)(lambda: gather(theirs, sol))
        copies = [pltpu.make_async_copy(sol, solved.at[1, :, cols], sems.at[steps])]
        copies[0].start()
        for i in range(steps):
            rows = slice(i * TILE, (i + 1) * TILE)
            old = cur[rows, cols]
            newer = (old.astype(F32) - scl[rows] * dot(pan[rows], sol[...])).astype(BF)
            tile[rows] = jnp.where(flags[0] > 1, newer, old)
            copy = pltpu.make_async_copy(tile.at[rows], out.at[rows, cols], sems.at[i])
            copy.start()
            copies.append(copy)
        for copy in copies:
            copy.wait()

    operands = [flags, current, scale, panel, *parts, *swapped, solved]
    aliases = {len(operands) - 1: 1}
    if remaining is not None:
        operands.append(remaining)
        aliases[len(operands) - 1] = 0
    return call(
        kernel,
        operands,
        [jax.ShapeDtypeStruct((n, n), BF), jax.ShapeDtypeStruct((2, half, n), BF)],
        [SMEM] + [VMEM] * (3 + 2 * pieces) + [ANY] * len(aliases),
        [ANY, ANY],
        [pltpu.VMEM((half, half), BF), pltpu.VMEM((n, half), BF), pltpu.SemaphoreType.DMA((steps + 1,))],
        aliases,
    )


def body(pending, panel, panel_scale, inverse_blocks):
    row, c = lax.axis_index("row"), lax.axis_index("col")
    z, x, k = lax.shift_right_logical(row, 2), lax.shift_right_logical(row, 1) & 1, row & 1
    half = inverse_blocks.shape[1]
    quarter = half // 2
    flags = jnp.stack([row, c, x, k]).astype(jnp.int32)
    flipped = jnp.stack([row, c, 1 - x, k]).astype(jnp.int32)
    roots = [((0, 0, 0, 0), (0, 1, 0, 0))]
    seconds = [((0, 0, 0, 1), (0, 1, 0, 1))]
    share, flags, flipped, near, middle, odd, outer, first_core = lax.optimization_barrier(
        (pending[:, 0, :], flags, flipped, x == 0, z == 2, (z & 1) == 1, z == 3, k == 0)
    )

    left = columns(share, 0)
    idle = [((0, c_, 0, 1), (0, c_, 1, 1)) for c_ in COLS] + [((0, c_, 1, 0), (1, c_, 1, 0)) for c_ in COLS]
    far_left = swap(left, roots + idle, "y")
    later, inverse = lax.optimization_barrier((share, inverse_blocks, left))[:2]
    rows = jnp.where(near, inverse[1, quarter:], inverse[1, :quarter])
    crossed = send(rows, [((1, 1, 0, 1), (1, 0, 0, 1)), ((0, 1, 1, 1), (0, 0, 1, 1))])
    panel0, panel1, later = lax.optimization_barrier((panel[:, 0, :], panel[:, 1, :], later))
    far_right = swap_some(columns(later, half), roots)
    far_top = send(crossed, [((1, 0, 0, 1), (0, 0, 0, 1))])
    far_bottom = send(crossed, [((0, 0, 1, 1), (0, 0, 0, 1))])
    scale0, scale1 = scale_columns(after(panel_scale.T, panel0))

    first_left = solve_first(flags, share, far_left, inverse, 0)
    left_here = core_swap(first_left)
    first_hop = send(first_left, [((0, c_, 0, 0), (1, c_, 0, 0)) for c_ in COLS])
    far_top, far_bottom = lax.optimization_barrier((far_top, far_bottom, first_left))[:2]
    own, message = second_block(flags, share, scale0, panel0, left_here, inverse, far_top, far_bottom, 0)

    first_right = solve_first(flags, share, after(far_right, own), inverse, half)
    own_hop = send(own, [((0, c_, 0, 1), (1, c_, 0, 1)) for c_ in COLS])
    inward = after(core_swap(first_right), first_hop)
    mine0 = lax.optimization_barrier(jnp.where(near, first_right, first_hop))
    outward = jnp.where(first_core, mine0, message)
    across = send(
        outward,
        [((x_, c_, 0, 0), (x_, c_, 2, 0)) for x_ in (0, 1) for c_ in COLS]
        + [((0, c_, 0, 1), (1, 1 - c_, 0, 1)) for c_ in COLS],
    )
    own, message = second_block(flags, share, scale0, after(panel0, outward), inward, inverse, far_top, far_bottom, half)
    answer = send(
        jnp.where(first_core, mine0, after(message, own_hop)),
        [((x_, c_, 0, 0), (x_, c_, 1, 0)) for x_ in (0, 1) for c_ in COLS]
        + [((0, c_, 0, 1), (0, 1 - c_, 0, 1)) for c_ in COLS],
    )
    last = send(after(across, message), [((x_, c_, 2, 0), (x_, c_, 3, 0)) for x_ in (0, 1) for c_ in COLS])

    second = solve_second(flags, (own, answer), (own_hop, across), inverse)

    rows = [slice(0, quarter), slice(quarter, half)]
    mine0 = jnp.where(odd, jnp.where(outer, last, answer), jnp.where(middle, across, mine0))
    far, heads, step, mine1, other1 = [], [], [], [], []
    for part, r in zip(second, rows):
        far.append(swap(jnp.where(first_core, mine0[r], part), far_step(1) + side_step(0), "y"))
    for part, head in zip(far, second):
        heads.append(jnp.where(middle, after(part, *heads), head))
        step.append(swap(heads[-1], near_step(1), "y"))
    for part, head in zip(step, heads):
        mine1.append(jnp.where(odd, after(part, *mine1), head))
        other1.append(swap(mine1[-1], side_step(1), "y"))
    mine0_here = core_swap(mine0)
    far_here = [core_swap(f) for f in far]

    current, solved = update_first(
        flags, share, scale0, panel0, ([mine0], [mine0_here]), (far, far_here)
    )
    remaining, solved = update_second(flipped, current, scale1, after(panel1, other1[0]), mine1, [core_swap(m) for m in mine1], solved)
    other1 = [after(m, remaining) for m in other1]
    remaining, solved = update_second(
        flags, current, scale1, panel1, other1, [core_swap(m) for m in other1], solved, remaining
    )
    return remaining[:, None, :], solved


def body_any(pending, panel, panel_scale, inverse_blocks):
    row = lax.axis_index("row")
    current = pending[:, 0, :]
    solved = []
    for k in range(2):
        fan = lax.psum(current, "col")
        local = dot(inverse_blocks[k], fan).astype(BF)
        arrived = lax.psum(jnp.where(row == k, local, jnp.zeros_like(local)), "row")
        solved.append(arrived)
        term = dot(panel[:, k, :], arrived)
        newer = (current.astype(F32) - panel_scale[:, k : k + 1] * term).astype(BF)
        current = jnp.where(row > k, newer, current)
    return current[:, None, :], jnp.stack(solved)


def solution(mesh):
    placed = (P("row", "col", None), P("row", None, "col"), P("row", None), P(None, "col", None))
    small = mesh.shape["row"] == 16 and mesh.shape["col"] == 2
    return jax.shard_map(
        body if small else body_any,
        mesh=mesh,
        in_specs=placed,
        out_specs=(P("row", "col", None), P(None, "col", None)),
        check_vma=False,
    )
```

```python
import jax
import jax.numpy as jnp
from jax import lax
from jax.experimental import pallas as pl
from jax.experimental.pallas import tpu as pltpu
from jax.sharding import PartitionSpec as P

AXES = ("row", "col")
BF = jnp.bfloat16
F32 = jnp.float32
VMEM_BYTES = 12 * 1024 * 1024
TILE = 256


def dot(a, b):
    return jnp.dot(a, b, preferred_element_type=F32)


def after(value, *others):
    return lax.optimization_barrier((value, *others))[0]


def device(x, c, z, k):
    return ((z * 2 + x) * 2 + k) * 2 + c


PLACES = [(x, c, z, k) for z in range(4) for x in range(2) for k in range(2) for c in range(2)]


def paired(wanted, side):
    mate = {}

    def join(a, b):
        assert a not in mate and b not in mate and a != b
        mate[a], mate[b] = b, a

    def across(place, axis):
        x, c, z, k = place
        return (1 - x, c, z, k) if axis == "x" else (x, 1 - c, z, k)

    def core(place):
        x, c, z, k = place
        return (x, c, z, 1 - k)

    for a, b in wanted:
        join(a, b)
    for axis in (side, "y" if side == "x" else "x"):
        for place in [p for p in PLACES if p not in mate and core(p) in mate]:
            if place not in mate and across(place, axis) not in mate:
                join(place, across(place, axis))
    for place in PLACES:
        if place not in mate:
            join(place, core(place))
    return [(device(*a), device(*b)) for a, b in mate.items()]


def swap(value, wanted, side):
    return lax.ppermute(value, AXES, paired(wanted, side))


def swap_some(value, wanted):
    return lax.ppermute(value, AXES, [(device(*p), device(*q)) for a, b in wanted for p, q in ((a, b), (b, a))])


def send(value, wanted):
    return lax.ppermute(value, AXES, [(device(*a), device(*b)) for a, b in wanted])


def core_swap(value):
    return swap(value, [((x, c, z, 0), (x, c, z, 1)) for x, c, z, k in PLACES if k == 0], "x")


COLS = (0, 1)


def far_step(core):
    return [((x, c, 0, core), (x, c, 2, core)) for c in COLS for x in (0, 1)]


def near_step(core):
    return [((x, c, z, core), (x, c, z + 1, core)) for c in COLS for x in (0, 1) for z in (0, 2)]


def side_step(core):
    return [((0, c, z, core), (1, c, z, core)) for c in COLS for z in range(4)]


VMEM = pl.BlockSpec(memory_space=pltpu.VMEM)
SMEM = pl.BlockSpec(memory_space=pltpu.SMEM)
ANY = pl.BlockSpec(memory_space=pl.ANY)


def call(kernel, operands, shapes, ins, outs, scratch=(), aliases=None):
    return pl.pallas_call(
        kernel,
        in_specs=ins,
        out_specs=outs,
        out_shape=shapes,
        scratch_shapes=list(scratch),
        input_output_aliases=aliases or {},
        compiler_params=pltpu.CompilerParams(vmem_limit_bytes=VMEM_BYTES),
    )(*operands)


def columns(share, start):
    n = share.shape[1]
    width, parts = n // 2, 4
    rows = n // parts

    def kernel(source, target, sems):
        copies = [
            pltpu.make_async_copy(
                source.at[pl.ds(i * rows, rows), pl.ds(start, width)], target.at[pl.ds(i * rows, rows)], sems.at[i]
            )
            for i in range(parts)
        ]
        for copy in copies:
            copy.start()
        for copy in copies:
            copy.wait()

    return call(
        kernel, (share,), jax.ShapeDtypeStruct((n, width), BF), [ANY], VMEM, [pltpu.SemaphoreType.DMA((parts,))]
    )


def solve_first(flags, share, far, inverse, start):
    half, n = inverse.shape[1:]

    def kernel(flags, cur, got, inv, out):
        @pl.when(flags[0] == 0)
        def _():
            for t in range(0, half, half):
                here = cur[:, start + t : start + t + half]
                fan = (here.astype(F32) + got[:, t : t + half].astype(F32)).astype(BF)
                out[:, t : t + half] = dot(inv[0], fan).astype(BF)

    return call(
        kernel, (flags, share, far, inverse), jax.ShapeDtypeStruct((half, half), BF), [SMEM] + [VMEM] * 3, VMEM
    )


def second_block(flags, share, scale, panel, solved, inverse, far_top, far_bottom, start):
    half, n = inverse.shape[1:]
    quarter = half // 2

    def kernel(flags, cur, scl, pan, sol, inv, top, bottom, own, message):
        @pl.when(flags[0] == 1)
        def _():
            for t in range(0, half, half):
                cols = slice(t, t + half)
                here = cur[:, start + t : start + t + half]
                newer = (here.astype(F32) - scl[...] * dot(pan[...], sol[:, cols])).astype(BF)

                @pl.when(flags[1] == 0)
                def _():
                    own[:, cols] = newer[:half]
                    message[:quarter, cols] = dot(top[...], newer).astype(BF)
                    message[quarter:, cols] = dot(bottom[...], newer).astype(BF)

                @pl.when(flags[1] != 0)
                def _():
                    own[:, cols] = dot(inv[1], newer).astype(BF)
                    message[:, cols] = newer[:half]

    return call(
        kernel,
        (flags, share, scale, panel, solved, inverse, far_top, far_bottom),
        [jax.ShapeDtypeStruct((half, half), BF)] * 2,
        [SMEM] + [VMEM] * 7,
        [VMEM] * 2,
    )


def solve_second(flags, right, left, inverse):
    half, n = inverse.shape[1:]
    quarter = half // 2

    def kernel(flags, a0, b0, a1, b1, inv, upper, lower, both):
        def one(a, b):
            both[...] = (a[...].astype(F32) + b[...].astype(F32)).astype(BF)

        pl.when(flags[0] == 1)(lambda: one(a0, b0))
        pl.when(flags[0] == 3)(lambda: one(a1, b1))
        here = jnp.logical_or(flags[0] == 1, flags[0] == 3)

        @pl.when(jnp.logical_and(flags[1] == 0, here))
        def _():
            upper[...] = dot(inv[1, :quarter, :half], both[...]).astype(BF)
            lower[...] = dot(inv[1, quarter:, :half], both[...]).astype(BF)

        @pl.when(jnp.logical_and(flags[1] != 0, here))
        def _():
            upper[...] = both[:quarter]
            lower[...] = both[quarter:]

    return call(
        kernel,
        (flags, *right, *left, inverse),
        [jax.ShapeDtypeStruct((quarter, half), BF)] * 2,
        [SMEM] + [VMEM] * 5,
        [VMEM] * 2,
        [pltpu.VMEM((half, half), BF)],
    )


def scale_columns(scale):
    n = scale.shape[1]

    def kernel(scl, first, second):
        both = jnp.transpose(jnp.concatenate([scl[...]] * 4))
        first[...] = both[:, 0:1]
        second[...] = both[:, 1:2]

    return call(kernel, (scale,), [jax.ShapeDtypeStruct((n, 1), F32)] * 2, [VMEM], [VMEM] * 2)


def gather(pieces, target):
    rows = target.shape[0] // len(pieces)
    for i, piece in enumerate(pieces):
        target[i * rows : (i + 1) * rows] = piece[...]


def update_first(flags, share, scale, panel, mine, other):
    n, half = panel.shape
    lists = [list(some) for pair in (mine, other) for some in pair]
    counts = [len(some) for some in lists]

    def kernel(flags, cur, scl, pan, *refs):
        refs = list(refs)
        parts = [[refs.pop(0) for _ in range(count)] for count in counts]
        out, solved, sol, sems = refs
        for at, side in ((0, 1 - flags[2]), (2, flags[2])):
            pl.when(flags[3] == 0)(lambda: gather(parts[at], sol.at[side]))
            pl.when(flags[3] != 0)(lambda: gather(parts[at + 1], sol.at[side]))
        copies = [
            pltpu.make_async_copy(sol.at[s], solved.at[0, :, pl.ds(s * half, half)], sems.at[s]) for s in range(2)
        ]
        for copy in copies:
            copy.start()
        for s in range(2):
            cols = slice(s * half, (s + 1) * half)
            for t in range(0, n, TILE):
                rows = slice(t, t + TILE)
                old = cur[rows, cols]
                newer = (old.astype(F32) - scl[rows] * dot(pan[rows], sol[s])).astype(BF)
                out[rows, cols] = jnp.where(flags[0] > 0, newer, old)
        for copy in copies:
            copy.wait()

    operands = [flags, share, scale, panel, *sum(lists, [])]
    return call(
        kernel,
        operands,
        [jax.ShapeDtypeStruct((n, n), BF), jax.ShapeDtypeStruct((2, half, n), BF)],
        [SMEM] + [VMEM] * (len(operands) - 1),
        [VMEM, ANY],
        [pltpu.VMEM((2, half, half), BF), pltpu.SemaphoreType.DMA((2,))],
    )


def update_second(flags, current, scale, panel, parts, swapped, solved, remaining=None):
    n, half = panel.shape
    steps = n // TILE
    pieces = len(parts)

    def kernel(flags, cur, scl, pan, *refs):
        mine, theirs = refs[:pieces], refs[pieces : 2 * pieces]
        out, solved, sol, tile, sems = refs[-5:]
        cols = pl.ds(pl.multiple_of(flags[2] * half, half), half)
        pl.when(flags[3] == 1)(lambda: gather(mine, sol))
        pl.when(flags[3] != 1)(lambda: gather(theirs, sol))
        copies = [pltpu.make_async_copy(sol, solved.at[1, :, cols], sems.at[steps])]
        copies[0].start()
        for i in range(steps):
            rows = slice(i * TILE, (i + 1) * TILE)
            old = cur[rows, cols]
            newer = (old.astype(F32) - scl[rows] * dot(pan[rows], sol[...])).astype(BF)
            tile[rows] = jnp.where(flags[0] > 1, newer, old)
            copy = pltpu.make_async_copy(tile.at[rows], out.at[rows, cols], sems.at[i])
            copy.start()
            copies.append(copy)
        for copy in copies:
            copy.wait()

    operands = [flags, current, scale, panel, *parts, *swapped, solved]
    aliases = {len(operands) - 1: 1}
    if remaining is not None:
        operands.append(remaining)
        aliases[len(operands) - 1] = 0
    return call(
        kernel,
        operands,
        [jax.ShapeDtypeStruct((n, n), BF), jax.ShapeDtypeStruct((2, half, n), BF)],
        [SMEM] + [VMEM] * (3 + 2 * pieces) + [ANY] * len(aliases),
        [ANY, ANY],
        [pltpu.VMEM((half, half), BF), pltpu.VMEM((n, half), BF), pltpu.SemaphoreType.DMA((steps + 1,))],
        aliases,
    )


def body(pending, panel, panel_scale, inverse_blocks):
    row, c = lax.axis_index("row"), lax.axis_index("col")
    z, x, k = lax.shift_right_logical(row, 2), lax.shift_right_logical(row, 1) & 1, row & 1
    half = inverse_blocks.shape[1]
    quarter = half // 2
    flags = jnp.stack([row, c, x, k]).astype(jnp.int32)
    flipped = jnp.stack([row, c, 1 - x, k]).astype(jnp.int32)
    roots = [((0, 0, 0, 0), (0, 1, 0, 0))]
    seconds = [((0, 0, 0, 1), (0, 1, 0, 1))]
    share, flags, flipped, near, middle, odd, outer, first_core = lax.optimization_barrier(
        (pending[:, 0, :], flags, flipped, x == 0, z == 2, (z & 1) == 1, z == 3, k == 0)
    )

    left = columns(share, 0)
    idle = [((0, c_, 0, 1), (0, c_, 1, 1)) for c_ in COLS] + [((0, c_, 1, 0), (1, c_, 1, 0)) for c_ in COLS]
    far_left = swap(left, roots + idle, "y")
    later, inverse = lax.optimization_barrier((share, inverse_blocks, left))[:2]
    rows = jnp.where(near, inverse[1, quarter:], inverse[1, :quarter])
    crossed = send(rows, [((1, 1, 0, 1), (1, 0, 0, 1)), ((0, 1, 1, 1), (0, 0, 1, 1))])
    panel0, panel1, later = lax.optimization_barrier((panel[:, 0, :], panel[:, 1, :], later))
    far_right = swap_some(columns(later, half), roots)
    far_top = send(crossed, [((1, 0, 0, 1), (0, 0, 0, 1))])
    far_bottom = send(crossed, [((0, 0, 1, 1), (0, 0, 0, 1))])
    scale0, scale1 = scale_columns(after(panel_scale.T, panel0))

    first_left = solve_first(flags, share, far_left, inverse, 0)
    left_here = core_swap(first_left)
    first_hop = send(first_left, [((0, c_, 0, 0), (1, c_, 0, 0)) for c_ in COLS])
    far_top, far_bottom = lax.optimization_barrier((far_top, far_bottom, first_left))[:2]
    own, message = second_block(flags, share, scale0, panel0, left_here, inverse, far_top, far_bottom, 0)

    first_right = solve_first(flags, share, after(far_right, own), inverse, half)
    own_hop = send(own, [((0, c_, 0, 1), (1, c_, 0, 1)) for c_ in COLS])
    inward = after(core_swap(first_right), first_hop)
    mine0 = lax.optimization_barrier(jnp.where(near, first_right, first_hop))
    outward = jnp.where(first_core, mine0, message)
    across = send(
        outward,
        [((x_, c_, 0, 0), (x_, c_, 2, 0)) for x_ in (0, 1) for c_ in COLS]
        + [((0, c_, 0, 1), (1, 1 - c_, 0, 1)) for c_ in COLS],
    )
    own, message = second_block(flags, share, scale0, after(panel0, outward), inward, inverse, far_top, far_bottom, half)
    answer = swap(
        jnp.where(first_core, mine0, after(message, own_hop)),
        seconds + [((x_, c_, 0, 0), (x_, c_, 1, 0)) for x_ in (0, 1) for c_ in COLS],
        "x",
    )
    last = send(after(across, message), [((x_, c_, 2, 0), (x_, c_, 3, 0)) for x_ in (0, 1) for c_ in COLS])

    second = solve_second(flags, (own, answer), (own_hop, across), inverse)

    rows = [slice(0, quarter), slice(quarter, half)]
    mine0 = jnp.where(odd, jnp.where(outer, last, answer), jnp.where(middle, across, mine0))
    far, heads, step, mine1, other1 = [], [], [], [], []
    for part, r in zip(second, rows):
        far.append(swap(jnp.where(first_core, mine0[r], part), far_step(1) + side_step(0), "y"))
    for part, head in zip(far, second):
        heads.append(jnp.where(middle, after(part, *heads), head))
        step.append(swap(heads[-1], near_step(1), "y"))
    for part, head in zip(step, heads):
        mine1.append(jnp.where(odd, after(part, *mine1), head))
        other1.append(swap(mine1[-1], side_step(1), "y"))
    mine0_here = core_swap(mine0)
    far_here = [core_swap(f) for f in far]

    current, solved = update_first(
        flags, share, scale0, panel0, ([mine0], [mine0_here]), (far, far_here)
    )
    remaining, solved = update_second(flipped, current, scale1, after(panel1, other1[0]), mine1, [core_swap(m) for m in mine1], solved)
    other1 = [after(m, remaining) for m in other1]
    remaining, solved = update_second(
        flags, current, scale1, panel1, other1, [core_swap(m) for m in other1], solved, remaining
    )
    return remaining[:, None, :], solved


def body_any(pending, panel, panel_scale, inverse_blocks):
    row = lax.axis_index("row")
    current = pending[:, 0, :]
    solved = []
    for k in range(2):
        fan = lax.psum(current, "col")
        local = dot(inverse_blocks[k], fan).astype(BF)
        arrived = lax.psum(jnp.where(row == k, local, jnp.zeros_like(local)), "row")
        solved.append(arrived)
        term = dot(panel[:, k, :], arrived)
        newer = (current.astype(F32) - panel_scale[:, k : k + 1] * term).astype(BF)
        current = jnp.where(row > k, newer, current)
    return current[:, None, :], jnp.stack(solved)


def solution(mesh):
    placed = (P("row", "col", None), P("row", None, "col"), P("row", None), P(None, "col", None))
    small = mesh.shape["row"] == 16 and mesh.shape["col"] == 2
    return jax.shard_map(
        body if small else body_any,
        mesh=mesh,
        in_specs=placed,
        out_specs=(P("row", "col", None), P(None, "col", None)),
        check_vma=False,
    )
```
